256 devices in a mesh: docs: 64 (over y_hi, x, z), dim: 4 (over y_lo, core).
Axes of the slice: x: 4, y: 4 (y_hi: 2, y_lo: 2; y = y_hi * 2 + y_lo), z: 8, core: 2. Of those that a mesh axis runs over, the one named last changes fastest.
Arguments:
- attn_in: bfloat16 [49152, 4096], P('docs', 'dim'), may hold values from -6 to 6
- out_grad: bfloat16 [49152, 4096], P('docs'), may hold values from -6 to 6
- o_weight: bfloat16 [4096, 4096], P('dim', 'docs'), may hold values from -0.09375 to 0.09375
- in_factor: bfloat16 [4096, 64], P('dim'), may hold values from -0.09375 to 0.09375
- out_factor: bfloat16 [4096, 64], replicated, may hold values from -0.09375 to 0.09375
- store: float32 [32768, 4096], P('docs', 'dim'), may hold values from -6 to 6
Outputs:
- in_cotangent: bfloat16 [49152, 4096], P('docs', 'dim')
- scores: float32 [192, 32768], P(None, 'docs')
The draws below stay inside these ranges and needn't reach their ends.
All inputs are finite; a program needn't handle non-finite values.
Results may differ from the reference program's by a relative error of at most 0.0004.
Values may be sent and summed in bfloat16 or wider, within the bound.
No kernel may reach another device: no remote copies, remote signals or barrier semaphores. Data moves between devices by JAX's collectives and lax.ppermute only.
A program may use at most 64 MiB of HBM per device.

```python
import jax
import jax.numpy as jnp
from jax import lax

D = 4096
RANK = 64
LENGTH = 256
K = 4096
TOKENS = 49152
DOCS = 32768


def shard_levels(stream_key, shape, split, least, top_value):
    loudness = 1.0
    for position, shards_of in split:
        steps = jax.random.uniform(jax.random.fold_in(jax.random.fold_in(stream_key, 6), position), (shards_of,), jnp.float32, least / len(split), top_value / len(split))
        loudness = loudness * jnp.repeat(jnp.exp(steps), shape[position] // shards_of).reshape((-1,) + (1,) * (len(shape) - 1 - position))
    return loudness


def bell_draw(own_key, extent, scale, most, shards=(), dtype=jnp.bfloat16):
    entries = scale * jax.random.normal(own_key, extent, jnp.float32)
    if shards:
        entries = entries * shard_levels(own_key, extent, shards, -0.22, 0.18)
    return jnp.clip(entries, -most, most).astype(dtype)


def setup_inputs(seed: int = 0) -> dict:
    key_list = jax.random.split(jax.random.key(seed), 7)
    return {
        "attn_in": bell_draw(key_list[0], (TOKENS, D), 1.0, 6.0, ((0, 64), (1, 4))),
        "out_grad": bell_draw(key_list[1], (TOKENS, D), 1.0, 6.0, ((0, 64),)),
        "o_weight": bell_draw(key_list[2], (D, D), D ** -0.5, 0.09375, ((0, 4), (1, 64))),
        "in_factor": bell_draw(key_list[3], (D, RANK), D ** -0.5, 0.09375, ((0, 4),)),
        "out_factor": bell_draw(key_list[4], (D, RANK), D ** -0.5, 0.09375),
        "store": bell_draw(key_list[5], (DOCS, K), 1.0, 6.0, ((0, 64), (1, 4)), jnp.float32),
    }


def reference(attn_in, out_grad, o_weight, in_factor, out_factor, store):
    in_cotangent = lax.dot_general(out_grad, o_weight, (((1,), (1,)), ((), ())), preferred_element_type=jnp.float32).astype(jnp.bfloat16)
    left = jnp.dot(attn_in, in_factor, preferred_element_type=jnp.float32)
    right = jnp.dot(out_grad, out_factor, preferred_element_type=jnp.float32)
    count = left.shape[0] // LENGTH
    left = left.reshape(count, LENGTH, RANK)
    right = right.reshape(count, LENGTH, RANK)
    projected = jnp.einsum('qlr,qls->qrs', left, right, precision=lax.Precision.HIGHEST).reshape(count, RANK * RANK)
    qscale = lax.rsqrt(lax.optimization_barrier(jnp.sum(projected * projected, axis=1)) + 1e-06)
    dscale = lax.rsqrt(lax.optimization_barrier(jnp.sum(store * store, axis=1)) + 1e-06)
    inner = lax.dot_general(projected, store, (((1,), (1,)), ((), ())), precision=lax.Precision.HIGHEST, preferred_element_type=jnp.float32)
    scores = inner * (float(RANK) * qscale[:, None]) * dscale[None, :]
    return (in_cotangent, scores)
```

```python
import jax
import jax.numpy as jnp
from jax import lax
from jax.sharding import Mesh
from jax.sharding import PartitionSpec as P

LENGTH = 256
NY, NX, NZ, NL, NC = 2, 4, 8, 2, 2
NAMES = ("yh", "x", "z", "yl", "core")
SIZES = dict(zip(NAMES, (NY, NX, NZ, NL, NC)))
DOCS = ("yh", "x", "z")
DIM = ("yl", "core")
CUT_A, CUT_B, CUT_C = 384, 384, 256


def fetch(value, **shift):
    axes = tuple(shift)
    sizes = [SIZES[axis] for axis in axes]
    pairs = []
    total = 1
    for size in sizes:
        total *= size
    for target in range(total):
        rest, place = target, []
        for size in reversed(sizes):
            place.append(rest % size)
            rest //= size
        place.reverse()
        source = 0
        for axis, size, at in zip(axes, sizes, place):
            source = source * size + (at + shift[axis]) % size
        pairs.append((source, target))
    return lax.ppermute(value, axes if len(axes) > 1 else axes[0], pairs)


def put(buffer, block, *starts):
    zero = jnp.int32(0)
    where = tuple(starts) + (zero,) * (buffer.ndim - len(starts))
    block = block.reshape((1,) * (buffer.ndim - block.ndim) + block.shape)
    return lax.dynamic_update_slice(buffer, block, where)


def weight_z_last(part, yh, x, z):
    depth, width = part.shape
    square = jnp.zeros((NY, NX, depth, width), part.dtype)
    for dy in range(NY):
        for dx in range(NX):
            if dy and dx:
                got = fetch(part, yh=dy, x=dx)
            elif dy:
                got = fetch(part, yh=dy)
            elif dx:
                got = fetch(part, x=dx)
            else:
                got = part
            square = put(square, got, (yh + dy) % NY, (x + dx) % NX)
    whole = jnp.zeros((NY, NX, NZ, depth, width), part.dtype)

    def store(whole, block, place):
        return lax.dynamic_update_slice(
            whole, block[:, :, None], (0, 0, (place + NZ) % NZ, 0, 0)
        )

    whole = store(whole, square, z)
    up = down = square
    for step in range(1, NZ // 2):
        up = fetch(up, z=1)
        down = fetch(down, z=-1)
        whole = store(whole, up, z + step)
        whole = store(whole, down, z - step)
    up = fetch(up[:1], z=1)
    down = fetch(down[1:], z=-1)
    whole = store(whole, jnp.concatenate([up, down], 0), z + NZ // 2)
    return whole.reshape(NY * NX * NZ * depth, width)


def weight_x_last(part, yh, x, z):
    depth, width = part.shape
    half = NZ // 2
    block = jnp.zeros((NY, 2, depth, width), part.dtype)
    high, low = z // half, z % half
    block = put(block, part, yh, high)
    block = put(block, fetch(part, yh=1), 1 - yh, high)
    block = put(block, fetch(part, z=half), yh, 1 - high)
    block = put(block, fetch(part, yh=1, z=half), 1 - yh, 1 - high)
    line = jnp.zeros((NY, 2, half, depth, width), part.dtype)

    def store_z(line, got, place):
        return lax.dynamic_update_slice(line, got[:, :, None], (0, 0, place % half, 0, 0))

    line = store_z(line, block, low)
    line = store_z(line, fetch(block, z=1), low + 1)
    line = store_z(line, fetch(block, z=-1), low + 3)
    far = jnp.concatenate([fetch(block[:1], z=2), fetch(block[1:], z=-2)], 0)
    line = store_z(line, far, low + 2)
    line = line.reshape(NY, NZ, depth, width)
    whole = jnp.zeros((NY, NX, NZ, depth, width), part.dtype)

    def store_x(whole, got, place):
        return lax.dynamic_update_slice(whole, got[:, None], (0, place % NX, 0, 0, 0))

    whole = store_x(whole, line, x)
    up, down = fetch(line, x=1), fetch(line, x=-1)
    whole = store_x(whole, up, x + 1)
    whole = store_x(whole, down, x + 3)
    far = jnp.concatenate([fetch(up[:1], x=1), fetch(down[1:], x=-1)], 0)
    whole = store_x(whole, far, x + 2)
    return whole.reshape(NY * NX * NZ * depth, width)


def weight_y_last(part, yh, x, z):
    depth, width = part.shape
    half = NZ // 2
    block = jnp.zeros((2, depth, width), part.dtype)
    high, low = z // half, z % half
    block = put(block, part, high)
    block = put(block, fetch(part, z=half), 1 - high)
    line = jnp.zeros((2, half, depth, width), part.dtype)

    def store_z(line, got, place):
        return lax.dynamic_update_slice(line, got[:, None], (0, place % half, 0, 0))

    line = store_z(line, block, low)
    line = store_z(line, fetch(block, z=1), low + 1)
    line = store_z(line, fetch(block, z=-1), low + 3)
    far = jnp.concatenate([fetch(block[:1], z=2), fetch(block[1:], z=-2)], 0)
    line = store_z(line, far, low + 2)
    line = line.reshape(NZ, depth, width)
    whole = jnp.zeros((NY, NX, NZ, depth, width), part.dtype)

    def store(whole, got, place):
        whole = put(whole, got, yh, place % NX)
        return put(whole, fetch(got, yh=1), 1 - yh, place % NX)

    whole = store(whole, line, x)
    up, down = fetch(line, x=1), fetch(line, x=-1)
    whole = store(whole, up, x + 1)
    whole = store(whole, down, x + 3)
    far = jnp.concatenate([fetch(up[: NZ // 2], x=1), fetch(down[NZ // 2 :], x=-1)], 0)
    whole = store(whole, far, x + 2)
    return whole.reshape(NY * NX * NZ * depth, width)


def all_rows_of(rows, yh, x, z):
    half = NZ // 2
    high, low = z // half, z % half
    block = jnp.zeros((NY, 2) + rows.shape, rows.dtype)
    block = put(block, rows, yh, high)
    block = put(block, fetch(rows, yh=1), 1 - yh, high)
    block = put(block, fetch(rows, z=half), yh, 1 - high)
    block = put(block, fetch(rows, yh=1, z=half), 1 - yh, 1 - high)
    line = jnp.zeros((NY, 2, half) + rows.shape, rows.dtype)

    def store_z(line, got, place):
        return lax.dynamic_update_slice(line, got[:, :, None], (0, 0, place % half, 0, 0))

    line = store_z(line, block, low)
    line = store_z(line, fetch(block, z=1), low + 1)
    line = store_z(line, fetch(block, z=-1), low + 3)
    far = jnp.concatenate([fetch(block[:1], z=2), fetch(block[1:], z=-2)], 0)
    line = store_z(line, far, low + 2)
    line = line.reshape((NY, NZ) + rows.shape)
    whole = jnp.zeros((NY, NX, NZ) + rows.shape, rows.dtype)

    def store_x(whole, got, place):
        return lax.dynamic_update_slice(whole, got[:, None], (0, place % NX, 0, 0, 0))

    whole = store_x(whole, line, x)
    whole = store_x(whole, fetch(line, x=1), x + 1)
    whole = store_x(whole, fetch(line, x=-1), x + 3)
    far = jnp.concatenate([fetch(line[:1], x=2), fetch(line[1:], x=-2)], 0)
    whole = store_x(whole, far, x + 2)
    return whole


def sum_over_dim(value):
    near = value + fetch(value, core=1)
    return near + fetch(near, yl=1)


def on_device(attn_in, out_grad, o_weight, in_factor, out_factor, store):
    yh, x, z = (lax.axis_index(axis) for axis in DOCS)
    core = lax.axis_index("core")
    tok_rows = out_grad.shape[0]
    rank_size = in_factor.shape[1]
    count = tok_rows // LENGTH
    share = store.shape[1]

    turned = o_weight.T
    part_a = turned[:, :CUT_A]
    part_b = turned[:, CUT_A : CUT_A + CUT_B]
    part_c = turned[:, CUT_A + CUT_B :]
    whole_a = weight_z_last(part_a, yh, x, z)
    whole_b = weight_x_last(part_b, yh, x, z)
    whole_c = weight_y_last(part_c, yh, x, z)

    right = jnp.dot(out_grad, out_factor, preferred_element_type=jnp.float32).reshape(
        count, LENGTH, rank_size
    )
    left = jnp.dot(attn_in, in_factor, preferred_element_type=jnp.float32).reshape(
        count, LENGTH, rank_size
    )
    partial_proj = jnp.einsum("qlr,qls->qrs", left, right, precision=lax.Precision.HIGHEST).reshape(
        count * rank_size * rank_size // 128, 128
    )
    full_proj = sum_over_dim(partial_proj).reshape(count, NL * NC, share // 128, 128)
    query_sq = jnp.sum(full_proj * full_proj, axis=(1, 2, 3))
    mine = lax.dynamic_index_in_dim(full_proj, lax.axis_index(DIM), 1, keepdims=False)
    unit_rows = mine * lax.rsqrt(query_sq + 1e-06)[:, None, None]
    all_rows = all_rows_of(unit_rows.reshape(count * share // 128, 128), yh, x, z)
    all_rows = all_rows.reshape(NY * NX * NZ * count, share)

    doc_sq = sum_over_dim(jnp.sum(store * store, axis=1))
    doc_scale = float(rank_size) * lax.rsqrt(doc_sq + 1e-06)
    partial_scores = lax.dot_general(
        all_rows,
        store,
        (((1,), (1,)), ((), ())),
        precision=lax.Precision.HIGH,
        preferred_element_type=jnp.float32,
    )
    half = partial_scores.shape[0] // NC
    kept = lax.dynamic_slice_in_dim(partial_scores, core * half, half, 0)
    given = lax.dynamic_slice_in_dim(partial_scores, (1 - core) * half, half, 0)
    kept = kept + fetch(given, core=1)
    kept = (kept + fetch(kept, yl=1)) * doc_scale[None, :]
    other = fetch(kept, core=1)
    scores = jnp.concatenate(
        [jnp.where(core == 0, kept, other), jnp.where(core == 0, other, kept)], 0
    )

    in_cotangent = jnp.concatenate(
        [
            jnp.dot(out_grad, whole, preferred_element_type=jnp.float32).astype(jnp.bfloat16)
            for whole in (whole_a, whole_b, whole_c)
        ],
        1,
    )
    return (in_cotangent, scores)


def solution(mesh):
    mesh = Mesh(mesh.devices.reshape(NY, NX, NZ, NL, NC), NAMES)
    placed = (
        P(DOCS, DIM),
        P(DOCS, None),
        P(DIM, DOCS),
        P(DIM, None),
        P(),
        P(DOCS, DIM),
    )
    return jax.shard_map(
        on_device,
        mesh=mesh,
        in_specs=placed,
        out_specs=(P(DOCS, DIM), P(None, DOCS)),
        check_vma=False,
    )
```

```python
import functools

import jax
import jax.numpy as jnp
from jax import lax
from jax.experimental import pallas as pl
from jax.experimental.pallas import tpu as pltpu
from jax.sharding import Mesh
from jax.sharding import PartitionSpec as P

LENGTH = 256
NY, NX, NZ, NL, NC = 2, 4, 8, 2, 2
NAMES = ("yh", "x", "z", "yl", "core")
SIZES = dict(zip(NAMES, (NY, NX, NZ, NL, NC)))
DOCS = ("yh", "x", "z")
DIM = ("yl", "core")
LANES = 128
NA, NB, NCC = 3, 3, 2
HOPS = (0, 1, -1, 2)


def fetch(value, **shift):
    ((axis, by),) = shift.items()
    size = SIZES[axis]
    return lax.ppermute(value, axis, [((to + by) % size, to) for to in range(size)])


def put(buffer, block, *starts):
    zero = jnp.int32(0)
    where = tuple(starts) + (zero,) * (buffer.ndim - len(starts))
    block = block.reshape((1,) * (buffer.ndim - block.ndim) + block.shape)
    return lax.dynamic_update_slice(buffer, block, where)


def all_rows_of(rows, yh, x, z):
    half = NZ // 2
    high, low = z // half, z % half
    block = jnp.zeros((NY,) + rows.shape, rows.dtype)
    block = put(block, rows, yh)
    block = put(block, fetch(rows, yh=1), 1 - yh)
    pair = jnp.zeros((NY, 2) + rows.shape, rows.dtype)

    def store_high(pair, got, place):
        return lax.dynamic_update_slice(pair, got[:, None], (0, place, 0, 0))

    pair = store_high(pair, block, high)
    pair = store_high(pair, fetch(block, z=half), 1 - high)
    line = jnp.zeros((NY, 2, half) + rows.shape, rows.dtype)

    def store_z(line, got, place):
        return lax.dynamic_update_slice(line, got[:, :, None], (0, 0, place % half, 0, 0))

    for hop in HOPS:
        line = store_z(line, fetch(pair, z=hop) if hop else pair, low + hop + half)
    line = line.reshape((NY, NZ) + rows.shape)
    whole = jnp.zeros((NY, NX, NZ) + rows.shape, rows.dtype)

    def store_x(whole, got, place):
        return lax.dynamic_update_slice(whole, got[:, None], (0, place % NX, 0, 0, 0))

    for hop in HOPS:
        whole = store_x(whole, fetch(line, x=hop) if hop else line, x + hop + NX)
    return whole


def place_and_multiply(groups, where, spot_ref, grad_ref, *refs):
    pieces, out_ref, weight = refs[:-2], refs[-2], refs[-1]
    yh, x, z = spot_ref[0], spot_ref[1], spot_ref[2]
    depth = pieces[0].shape[1]
    for piece, blocks in zip(pieces, where):
        for j, (dy, dx, dz, moved, group) in enumerate(blocks):
            at_z = (z + (dz + NZ)) % NZ if moved else dz
            shard = (((yh + dy) % NY) * NX + (x + (dx + NX)) % NX) * NZ + at_z
            rows = pl.ds(pl.multiple_of(shard * depth, depth), depth)
            weight[rows, group * LANES : (group + 1) * LANES] = piece[j]
    step = 256
    for start in range(0, grad_ref.shape[0], step):
        out_ref[start : start + step, :] = jnp.dot(
            grad_ref[start : start + step, :], weight[...], preferred_element_type=jnp.float32
        ).astype(out_ref.dtype)


def multiply(spot, out_grad, pieces, where, groups):
    rows, depth = out_grad.shape
    width = groups * LANES
    return pl.pallas_call(
        functools.partial(place_and_multiply, groups, where),
        out_shape=jax.ShapeDtypeStruct((rows, width), out_grad.dtype),
        in_specs=[pl.BlockSpec(memory_space=pltpu.SMEM)]
        + [pl.BlockSpec(memory_space=pltpu.VMEM)] * (1 + len(pieces)),
        out_specs=pl.BlockSpec(memory_space=pltpu.VMEM),
        scratch_shapes=[pltpu.VMEM((depth, width), out_grad.dtype)],
        compiler_params=pltpu.CompilerParams(vmem_limit_bytes=40 * 1024 * 1024),
        cost_estimate=pl.CostEstimate(
            flops=2 * rows * depth * width,
            bytes_accessed=2 * (rows * depth + depth * width + rows * width),
            transcendentals=0,
        ),
    )(spot, out_grad, *pieces)


def on_device(attn_in, out_grad, o_weight, in_factor, out_factor, store):
    yh, x, z = (lax.axis_index(axis) for axis in DOCS)
    core = lax.axis_index("core")
    tok_rows = out_grad.shape[0]
    rank_size = in_factor.shape[1]
    count = tok_rows // LENGTH
    share = store.shape[1]
    depth = o_weight.shape[1]
    shards = jnp.swapaxes(o_weight.T.reshape(depth, -1, LANES), 0, 1)

    part_a = shards[:NA]
    pair_a = jnp.concatenate([part_a, fetch(part_a, yh=1)], 0)
    square = jnp.concatenate([fetch(pair_a, x=hop) if hop else pair_a for hop in HOPS], 0)
    whole_a = lax.all_gather(square, "z", axis=0, tiled=True)
    where_a = [
        (dy, dx, at, False, group)
        for at in range(NZ)
        for dx in HOPS
        for dy in range(NY)
        for group in range(NA)
    ]

    part = shards[NA:]
    pair = jnp.stack([part, fetch(part, z=NZ // 2)], 0)
    line = jnp.stack([fetch(pair, z=hop) if hop else pair for hop in HOPS], 0)

    def flat(value):
        return value.reshape((-1,) + value.shape[-2:])

    line_c = line[:, :, NB:]
    pieces_c = [line_c] + [fetch(line_c, x=hop) for hop in HOPS[1:]]
    pieces_c = [flat(piece) for piece in pieces_c + [fetch(piece, yh=1) for piece in pieces_c]]
    where_c = [
        [
            (dy, dx, dz + dh * (NZ // 2), True, NB + group)
            for dz in HOPS
            for dh in range(2)
            for group in range(NCC)
        ]
        for dy in range(NY)
        for dx in HOPS
    ]

    line_b = line[:, :, :NB]
    both_b = jnp.stack([line_b, fetch(line_b, yh=1)], 0)
    up, down = fetch(both_b, x=1), fetch(both_b, x=-1)
    far_up, far_down = fetch(up[:1], x=1), fetch(down[1:], x=-1)
    pieces_b = [flat(piece) for piece in (both_b, up, down, far_up, far_down)]
    where_b = [
        [
            (dy, dx, dz + dh * (NZ // 2), True, group)
            for dy in sides
            for dz in HOPS
            for dh in range(2)
            for group in range(NB)
        ]
        for dx, sides in ((0, (0, 1)), (1, (0, 1)), (-1, (0, 1)), (2, (0,)), (2, (1,)))
    ]

    right = jnp.dot(out_grad, out_factor, preferred_element_type=jnp.float32).reshape(
        count, LENGTH, rank_size
    )
    left = jnp.dot(attn_in, in_factor, preferred_element_type=jnp.float32).reshape(
        count, LENGTH, rank_size
    )
    partial_proj = jnp.einsum("qlr,qls->qrs", left, right, precision=lax.Precision.HIGHEST).reshape(
        count * rank_size * rank_size // LANES, LANES
    )
    full_proj = partial_proj + fetch(partial_proj, core=1)
    full_proj = full_proj + fetch(full_proj, yl=1)
    full_proj = full_proj.reshape(count, NL * NC, share // LANES, LANES)
    query_sq = jnp.sum(full_proj * full_proj, axis=(1, 2, 3))
    mine = lax.dynamic_index_in_dim(full_proj, lax.axis_index(DIM), 1, keepdims=False)
    unit_rows = mine * lax.rsqrt(query_sq + 1e-06)[:, None, None]
    all_rows = all_rows_of(unit_rows.reshape(count * share // LANES, LANES), yh, x, z)
    all_rows = all_rows.reshape(NY * NX * NZ * count, share)

    doc_sq = jnp.sum(store * store, axis=1)
    partial_scores = lax.dot_general(
        all_rows,
        store,
        (((1,), (1,)), ((), ())),
        precision=lax.Precision.HIGH,
        preferred_element_type=jnp.float32,
    )
    half = partial_scores.shape[0] // NC
    norm_rows = jnp.broadcast_to(doc_sq[None, :], (8, doc_sq.shape[0]))
    kept = lax.dynamic_slice_in_dim(partial_scores, core * half, half, 0)
    given = lax.dynamic_slice_in_dim(partial_scores, (1 - core) * half, half, 0)
    kept = jnp.concatenate([kept, norm_rows], 0)
    given = jnp.concatenate([given, norm_rows], 0)
    kept = kept + fetch(given, core=1)
    kept = kept + fetch(kept, yl=1)
    kept = kept[:half] * (float(rank_size) * lax.rsqrt(kept[half] + 1e-06))[None, :]
    other = fetch(kept, core=1)
    scores = jnp.concatenate(
        [jnp.where(core == 0, kept, other), jnp.where(core == 0, other, kept)], 0
    )

    spot = jnp.stack([yh, x, z]).astype(jnp.int32)
    in_cotangent = jnp.concatenate(
        [
            multiply(spot, out_grad, [whole_a], [where_a], NA),
            multiply(spot, out_grad, pieces_b + pieces_c, where_b + where_c, NB + NCC),
        ],
        1,
    )
    return (in_cotangent, scores)


def solution(mesh):
    mesh = Mesh(mesh.devices.reshape(NY, NX, NZ, NL, NC), NAMES)
    placed = (
        P(DOCS, DIM),
        P(DOCS, None),
        P(DIM, DOCS),
        P(DIM, None),
        P(),
        P(DOCS, DIM),
    )
    return jax.shard_map(
        on_device,
        mesh=mesh,
        in_specs=placed,
        out_specs=(P(DOCS, DIM), P(None, DOCS)),
        check_vma=False,
    )
```

```python
import functools

import jax
import jax.numpy as jnp
from jax import lax
from jax.experimental import pallas as pl
from jax.experimental.pallas import tpu as pltpu
from jax.sharding import Mesh
from jax.sharding import PartitionSpec as P

LENGTH = 256
NY, NX, NZ, NL, NC = 2, 4, 8, 2, 2
NAMES = ("yh", "x", "z", "yl", "core")
SIZES = dict(zip(NAMES, (NY, NX, NZ, NL, NC)))
DOCS = ("yh", "x", "z")
DIM = ("yl", "core")
LANES = 128
HALF_Z = NZ // 2


def fetch(value, **shift):
    ((axis, by),) = shift.items()
    size = SIZES[axis]
    return lax.ppermute(value, axis, [((to + by) % size, to) for to in range(size)])


def put(buffer, block, *starts):
    zero = jnp.int32(0)
    where = tuple(starts) + (zero,) * (buffer.ndim - len(starts))
    block = block.reshape((1,) * (buffer.ndim - block.ndim) + block.shape)
    return lax.dynamic_update_slice(buffer, block, where)


def around(block, axis):
    return [block, fetch(block, **{axis: 1}), fetch(block, **{axis: 2}), fetch(block, **{axis: -1})]


def ring(line, axis):
    half = line.shape[0] // 2
    up, down = fetch(line, **{axis: 1}), fetch(line, **{axis: -1})
    far_up = fetch(up[:half], **{axis: 1})
    far_down = fetch(down[half:], **{axis: -1})
    return [line, up, far_up, far_down, down]


def all_rows_of(rows, yh, x, z):
    high, low = z // HALF_Z, z % HALF_Z
    pair = jnp.zeros((2,) + rows.shape, rows.dtype)
    pair = put(pair, rows, high)
    pair = put(pair, fetch(rows, z=HALF_Z), 1 - high)
    both = jnp.zeros((NY,) + pair.shape, rows.dtype)
    both = put(both, pair, yh)
    both = put(both, fetch(pair, yh=1), 1 - yh)
    line = jnp.zeros((NY, 2, HALF_Z) + rows.shape, rows.dtype)
    for hop, got in enumerate(around(both, "z")):
        line = lax.dynamic_update_slice(
            line, got[:, :, None], (0, 0, (low + hop) % HALF_Z, 0, 0)
        )
    line = line.reshape((NY, NZ) + rows.shape)
    whole = jnp.zeros((NY, NX, NZ) + rows.shape, rows.dtype)
    for hop, got in enumerate(around(line, "x")):
        whole = lax.dynamic_update_slice(whole, got[:, None], (0, (x + hop) % NX, 0, 0, 0))
    return whole


def place_and_multiply(where, spot_ref, grad_ref, *refs):
    pieces, out_ref, weight = refs[:-2], refs[-2], refs[-1]
    yh, x, z = spot_ref[0], spot_ref[1], spot_ref[2]
    depth = pieces[0].shape[1]
    for piece, (first, other, along) in zip(pieces, where):

        @pl.loop(0, piece.shape[0])
        def _(i):
            hop = first + i // 4
            dx, dz = (hop, other) if along == "x" else (other, hop + HALF_Z * (hop // 3))
            at_y = (yh + (i // 2) % 2) % NY
            at_z = (z + dz + (i % 2) * HALF_Z) % NZ
            shard = (at_y * NX + (x + dx) % NX) * NZ + at_z
            weight[pl.ds(pl.multiple_of(shard * depth, depth), depth), :] = piece[i]

    step = 256

    @pl.loop(0, grad_ref.shape[0] // step)
    def _(i):
        rows = pl.ds(pl.multiple_of(i * step, step), step)
        out_ref[rows, :] = jnp.dot(
            grad_ref[rows, :], weight[...], preferred_element_type=jnp.float32
        ).astype(out_ref.dtype)


def multiply(spot, out_grad, pieces, where):
    rows, depth = out_grad.shape
    width = pieces[0].shape[-1]
    return pl.pallas_call(
        functools.partial(place_and_multiply, where),
        out_shape=jax.ShapeDtypeStruct((rows, width), out_grad.dtype),
        in_specs=[pl.BlockSpec(memory_space=pltpu.SMEM)]
        + [pl.BlockSpec(memory_space=pltpu.VMEM)] * (1 + len(pieces)),
        out_specs=pl.BlockSpec(memory_space=pltpu.VMEM),
        scratch_shapes=[pltpu.VMEM((depth, width), out_grad.dtype)],
        compiler_params=pltpu.CompilerParams(vmem_limit_bytes=40 * 1024 * 1024),
        cost_estimate=pl.CostEstimate(
            flops=2 * rows * depth * width,
            bytes_accessed=2 * (rows * depth + depth * width + rows * width),
            transcendentals=0,
        ),
    )(spot, out_grad, *pieces)


def on_device(attn_in, out_grad, o_weight, in_factor, out_factor, store):
    yh, x, z = (lax.axis_index(axis) for axis in DOCS)
    core = lax.axis_index("core")
    tok_rows = out_grad.shape[0]
    rank_size = in_factor.shape[1]
    count = tok_rows // LENGTH
    share = store.shape[1]
    shard = o_weight.T
    half_width = shard.shape[1] // 2
    pair = jnp.stack([shard, fetch(shard, z=HALF_Z)], 0)
    both = jnp.concatenate([pair, fetch(pair, yh=1)], 0)
    line_a = jnp.concatenate(around(both[..., :half_width], "x"), 0)
    line_b = jnp.concatenate(around(both[..., half_width:], "z"), 0)
    pieces_a = ring(line_a, "z")
    pieces_b = ring(line_b, "x")
    where_a = [(0, 0, "x"), (0, 1, "x"), (0, 2, "x"), (2, NZ - 2, "x"), (0, NZ - 1, "x")]
    where_b = [(0, 0, "z"), (0, 1, "z"), (0, 2, "z"), (2, NX - 2, "z"), (0, NX - 1, "z")]

    right = jnp.dot(out_grad, out_factor, preferred_element_type=jnp.float32).reshape(
        count, LENGTH, rank_size
    )
    left = jnp.dot(attn_in, in_factor, preferred_element_type=jnp.float32).reshape(
        count, LENGTH, rank_size
    )
    partial_proj = jnp.einsum("qlr,qls->qrs", left, right, precision=lax.Precision.HIGHEST).reshape(
        count * rank_size * rank_size // LANES, LANES
    )
    full_proj = partial_proj + fetch(partial_proj, core=1)
    full_proj = full_proj + fetch(full_proj, yl=1)
    full_proj = full_proj.reshape(count, NL * NC, share // LANES, LANES)
    query_sq = jnp.sum(full_proj * full_proj, axis=(1, 2, 3))
    mine = lax.dynamic_index_in_dim(full_proj, lax.axis_index(DIM), 1, keepdims=False)
    unit_rows = mine * lax.rsqrt(query_sq + 1e-06)[:, None, None]
    all_rows = all_rows_of(unit_rows.reshape(count * share // LANES, LANES), yh, x, z)
    all_rows = all_rows.reshape(NY * NX * NZ * count, share)

    doc_sq = jnp.sum(store * store, axis=1)
    partial_scores = lax.dot_general(
        all_rows,
        store,
        (((1,), (1,)), ((), ())),
        precision=lax.Precision.HIGH,
        preferred_element_type=jnp.float32,
    )
    half = partial_scores.shape[0] // NC
    norm_rows = jnp.broadcast_to(doc_sq[None, :], (8, doc_sq.shape[0]))
    kept = lax.dynamic_slice_in_dim(partial_scores, core * half, half, 0)
    given = lax.dynamic_slice_in_dim(partial_scores, (1 - core) * half, half, 0)
    kept = jnp.concatenate([kept, norm_rows], 0)
    given = jnp.concatenate([given, norm_rows], 0)
    kept = kept + fetch(given, core=1)
    kept = kept + fetch(kept, yl=1)
    kept = kept[:half] * (float(rank_size) * lax.rsqrt(kept[half] + 1e-06))[None, :]
    other = fetch(kept, core=1)
    scores = jnp.concatenate(
        [jnp.where(core == 0, kept, other), jnp.where(core == 0, other, kept)], 0
    )

    spot = jnp.stack([yh, x, z]).astype(jnp.int32)
    in_cotangent = jnp.concatenate(
        [
            multiply(spot, out_grad, pieces_a, where_a),
            multiply(spot, out_grad, pieces_b, where_b),
        ],
        1,
    )
    return (in_cotangent, scores)


def solution(mesh):
    mesh = Mesh(mesh.devices.reshape(NY, NX, NZ, NL, NC), NAMES)
    placed = (
        P(DOCS, DIM),
        P(DOCS, None),
        P(DIM, DOCS),
        P(DIM, None),
        P(),
        P(DOCS, DIM),
    )
    return jax.shard_map(
        on_device,
        mesh=mesh,
        in_specs=placed,
        out_specs=(P(DOCS, DIM), P(None, DOCS)),
        check_vma=False,
    )
```

```python
import functools

import jax
import jax.numpy as jnp
from jax import lax
from jax.experimental import pallas as pl
from jax.experimental.pallas import tpu as pltpu
from jax.sharding import Mesh
from jax.sharding import PartitionSpec as P

LENGTH = 256
NY, NX, NZ, NL, NC = 2, 4, 8, 2, 2
NAMES = ("yh", "x", "z", "yl", "core")
SIZES = dict(zip(NAMES, (NY, NX, NZ, NL, NC)))
DOCS = ("yh", "x", "z")
DIM = ("yl", "core")
LANES = 128
HALF_Z = NZ // 2


def fetch(value, **shift):
    ((axis, by),) = shift.items()
    size = SIZES[axis]
    return lax.ppermute(value, axis, [((to + by) % size, to) for to in range(size)])


def put(buffer, block, *starts):
    zero = jnp.int32(0)
    where = tuple(starts) + (zero,) * (buffer.ndim - len(starts))
    block = block.reshape((1,) * (buffer.ndim - block.ndim) + block.shape)
    return lax.dynamic_update_slice(buffer, block, where)


def around(block, axis):
    return [block, fetch(block, **{axis: 1}), fetch(block, **{axis: 2}), fetch(block, **{axis: -1})]


def rows_over_z(rows, yh, z):
    high, low = z // HALF_Z, z % HALF_Z
    pair = jnp.zeros((2,) + rows.shape, rows.dtype)
    pair = put(pair, rows, high)
    pair = put(pair, fetch(rows, z=HALF_Z), 1 - high)
    both = jnp.zeros((NY,) + pair.shape, rows.dtype)
    both = put(both, pair, yh)
    both = put(both, fetch(pair, yh=1), 1 - yh)
    line = jnp.zeros((NY, 2, HALF_Z) + rows.shape, rows.dtype)
    for hop, got in enumerate(around(both, "z")):
        line = lax.dynamic_update_slice(
            line, got[:, :, None], (0, 0, (low + hop) % HALF_Z, 0, 0)
        )
    return line.reshape((NY, NZ) + rows.shape)


def rows_over_x(line, x):
    whole = jnp.zeros((NY, NX) + line.shape[1:], line.dtype)
    for hop, got in enumerate(around(line, "x")):
        whole = lax.dynamic_update_slice(whole, got[:, None], (0, (x + hop) % NX, 0, 0, 0))
    return whole


def by_class(spot_ref, grad_ref, out_ref):
    z = spot_ref[2]
    rows = grad_ref.shape[0]
    depth = LANES // 2
    low_lane = lax.broadcasted_iota(jnp.int32, (rows, LANES), 1) < depth

    def swapped(tile):
        return jnp.concatenate([tile[:, depth:], tile[:, :depth]], 1)

    for place, hop in enumerate((0, 1, 3, 2)):
        kind = (z + hop) % HALF_Z
        odd = kind % 2

        @pl.loop(0, NY * NX)
        def _(group):
            start = group * NZ * depth + (kind // 2) * LANES
            near = grad_ref[:, pl.ds(pl.multiple_of(start, LANES), LANES)]
            far = grad_ref[:, pl.ds(pl.multiple_of(start + 2 * LANES, LANES), LANES)]
            even_tile = jnp.where(low_lane, near, swapped(far))
            odd_tile = jnp.where(low_lane, swapped(near), far)
            to = place * NY * NX * LANES + group * LANES
            out_ref[:, pl.ds(pl.multiple_of(to, LANES), LANES)] = jnp.where(
                odd == 1, odd_tile, even_tile
            )


def place(weight, piece, spot_ref, along, first, hop):
    yh, x, z = spot_ref[0], spot_ref[1], spot_ref[2]
    depth = piece.shape[1]

    @pl.loop(0, piece.shape[0])
    def _(i):
        other = first + i // 4
        at_y = (yh + (i // 2) % 2) % NY
        if along == "z":
            at_z = (z + (hop + NZ) + (i % 2) * HALF_Z) % NZ
            shard = (at_y * NX + (x + other) % NX) * 2 + at_z // HALF_Z
        else:
            at_z = (z + other + (other // 3 + i % 2) * HALF_Z) % NZ
            shard = at_y * NZ + at_z
        weight[pl.ds(pl.multiple_of(shard * depth, depth), depth), :] = piece[i]


STEP = 256


def class_product(grad_ref, rows, weight, spot_ref, along, hop):
    depth = weight.shape[0]
    if along == "z":
        start = (0, 1, -1, 2).index(hop) * depth
        return jnp.dot(
            grad_ref[rows, start : start + depth], weight[...], preferred_element_type=jnp.float32
        )
    half = depth // NY
    total = None
    for at_y in range(NY):
        start = (at_y * NX + (spot_ref[1] + (hop + NX)) % NX) * half
        part = jnp.dot(
            grad_ref[rows, pl.ds(pl.multiple_of(start, half), half)],
            weight[at_y * half : (at_y + 1) * half, :],
            preferred_element_type=jnp.float32,
        )
        total = part if total is None else total + part
    return total


def near_part(along, spot_ref, grad_ref, own_ref, up_ref, down_ref, sum_ref, weight):
    for index, (piece, hop) in enumerate(((own_ref, 0), (up_ref, 1), (down_ref, -1))):
        place(weight, piece, spot_ref, along, 0, hop)

        @pl.loop(0, grad_ref.shape[0] // STEP)
        def _(i):
            rows = pl.ds(pl.multiple_of(i * STEP, STEP), STEP)
            part = class_product(grad_ref, rows, weight, spot_ref, along, hop)
            sum_ref[rows, :] = part if index == 0 else sum_ref[rows, :] + part


def far_part(spot_ref, *refs):
    out_ref, weight = refs[-2:]
    width = weight.shape[1]
    for index, along in enumerate(("z", "x")):
        grad_ref, sum_ref, up_ref, down_ref = refs[4 * index : 4 * index + 4]
        place(weight, up_ref, spot_ref, along, 0, 2)
        place(weight, down_ref, spot_ref, along, 2, -2)

        @pl.loop(0, grad_ref.shape[0] // STEP)
        def _(i):
            rows = pl.ds(pl.multiple_of(i * STEP, STEP), STEP)
            part = class_product(grad_ref, rows, weight, spot_ref, along, 2)
            out_ref[rows, index * width : (index + 1) * width] = (sum_ref[rows, :] + part).astype(
                out_ref.dtype
            )


def on_core(kernel, out_shape, spot, operands, scratch=(), flops=0):
    moved = sum(x.size * x.dtype.itemsize for x in operands)
    return pl.pallas_call(
        kernel,
        out_shape=out_shape,
        in_specs=[pl.BlockSpec(memory_space=pltpu.SMEM)]
        + [pl.BlockSpec(memory_space=pltpu.VMEM)] * len(operands),
        out_specs=pl.BlockSpec(memory_space=pltpu.VMEM),
        scratch_shapes=list(scratch),
        compiler_params=pltpu.CompilerParams(vmem_limit_bytes=40 * 1024 * 1024),
        cost_estimate=pl.CostEstimate(flops=flops, bytes_accessed=moved, transcendentals=0),
    )(spot, *operands)


def on_device(attn_in, out_grad, o_weight, in_factor, out_factor, store):
    yh, x, z = (lax.axis_index(axis) for axis in DOCS)
    core = lax.axis_index("core")
    tok_rows = out_grad.shape[0]
    rank_size = in_factor.shape[1]
    count = tok_rows // LENGTH
    share = store.shape[1]
    half_width = o_weight.shape[0] // 2
    spot = jnp.stack([yh, x, z]).astype(jnp.int32)

    shard = o_weight.T
    other = fetch(shard, z=HALF_Z)
    right = jnp.dot(out_grad, out_factor, preferred_element_type=jnp.float32).reshape(
        count, LENGTH, rank_size
    )
    left = jnp.dot(attn_in, in_factor, preferred_element_type=jnp.float32).reshape(
        count, LENGTH, rank_size
    )
    partial_proj = jnp.einsum("qlr,qls->qrs", left, right, precision=lax.Precision.HIGHEST).reshape(
        count * rank_size * rank_size // LANES, LANES
    )
    partial_proj, other = lax.optimization_barrier((partial_proj, other))

    pair = jnp.stack([shard, other], 0)
    both = jnp.concatenate([pair, fetch(pair, yh=1)], 0)
    full_proj = partial_proj + fetch(partial_proj, core=1)
    full_proj = full_proj + fetch(full_proj, yl=1)
    full_proj = full_proj.reshape(count, NL * NC, share // LANES, LANES)
    query_sq = jnp.sum(full_proj * full_proj, axis=(1, 2, 3))
    mine = lax.dynamic_index_in_dim(full_proj, lax.axis_index(DIM), 1, keepdims=False)
    unit_rows = mine * lax.rsqrt(query_sq + 1e-06)[:, None, None]
    unit_rows, both = lax.optimization_barrier((unit_rows, both))

    line_a = jnp.concatenate(around(both[..., :half_width], "x"), 0)
    line_b = jnp.concatenate(around(both[..., half_width:], "z"), 0)
    rows = rows_over_z(unit_rows.reshape(count * share // LANES, LANES), yh, z)
    ordered = on_core(by_class, jax.ShapeDtypeStruct(out_grad.shape, out_grad.dtype), spot, [out_grad])
    doc_sq = jnp.sum(store * store, axis=1)
    rows, line_a, line_b, ordered, doc_sq = lax.optimization_barrier(
        (rows, line_a, line_b, ordered, doc_sq)
    )

    up_a, down_a = fetch(line_a, z=1), fetch(line_a, z=-1)
    up_b, down_b = fetch(line_b, x=1), fetch(line_b, x=-1)
    all_rows = rows_over_x(rows, x).reshape(NY * NX * NZ * count, share)
    partial_scores = lax.dot_general(
        all_rows,
        store,
        (((1,), (1,)), ((), ())),
        precision=lax.Precision.HIGH,
        preferred_element_type=jnp.float32,
    )
    half = partial_scores.shape[0] // NC
    norm_rows = jnp.broadcast_to(doc_sq[None, :], (8, doc_sq.shape[0]))
    kept = lax.dynamic_slice_in_dim(partial_scores, core * half, half, 0)
    given = lax.dynamic_slice_in_dim(partial_scores, (1 - core) * half, half, 0)
    kept = jnp.concatenate([kept, norm_rows], 0)
    given = jnp.concatenate([given, norm_rows], 0)
    kept = kept + fetch(given, core=1)
    kept = kept + fetch(kept, yl=1)
    kept = kept[:half] * (float(rank_size) * lax.rsqrt(kept[half] + 1e-06))[None, :]
    kept, up_a, down_a, up_b, down_b = lax.optimization_barrier((kept, up_a, down_a, up_b, down_b))

    middle = line_a.shape[0] // 2
    far_a = [fetch(up_a[:middle], z=1), fetch(down_a[middle:], z=-1)]
    far_b = [fetch(up_b[:middle], x=1), fetch(down_b[middle:], x=-1)]
    other = fetch(kept, core=1)
    scores = jnp.concatenate(
        [jnp.where(core == 0, kept, other), jnp.where(core == 0, other, kept)], 0
    )
    weight = pltpu.VMEM((out_grad.shape[1] // 4, half_width), out_grad.dtype)
    sums = jax.ShapeDtypeStruct((tok_rows, half_width), jnp.float32)
    flops = 2 * tok_rows * out_grad.shape[1] * half_width
    sum_a, sum_b = (
        on_core(functools.partial(near_part, along), sums, spot, operands, [weight], flops * 3 // 4)
        for along, operands in (
            ("z", [ordered, line_a, up_a, down_a]),
            ("x", [out_grad, line_b, up_b, down_b]),
        )
    )
    in_cotangent = on_core(
        far_part,
        jax.ShapeDtypeStruct((tok_rows, 2 * half_width), out_grad.dtype),
        spot,
        [ordered, sum_a] + far_a + [out_grad, sum_b] + far_b,
        [weight],
        flops // 2,
    )
    return (in_cotangent, scores)


def solution(mesh):
    mesh = Mesh(mesh.devices.reshape(NY, NX, NZ, NL, NC), NAMES)
    placed = (
        P(DOCS, DIM),
        P(DOCS, None),
        P(DIM, DOCS),
        P(DIM, None),
        P(),
        P(DOCS, DIM),
    )
    return jax.shard_map(
        on_device,
        mesh=mesh,
        in_specs=placed,
        out_specs=(P(DOCS, DIM), P(None, DOCS)),
        check_vma=False,
    )
```

```python
import functools

import jax
import jax.numpy as jnp
from jax import lax
from jax.experimental import pallas as pl
from jax.experimental.pallas import tpu as pltpu
from jax.sharding import Mesh
from jax.sharding import PartitionSpec as P

LENGTH = 256
NY, NX, NZ, NL, NC = 2, 4, 8, 2, 2
NAMES = ("yh", "x", "z", "yl", "core")
SIZES = dict(zip(NAMES, (NY, NX, NZ, NL, NC)))
DOCS = ("yh", "x", "z")
DIM = ("yl", "core")
LANES = 128
HALF_Z = NZ // 2


def fetch(value, **shift):
    ((axis, by),) = shift.items()
    size = SIZES[axis]
    return lax.ppermute(value, axis, [((to + by) % size, to) for to in range(size)])


def put(buffer, block, *starts):
    zero = jnp.int32(0)
    where = tuple(starts) + (zero,) * (buffer.ndim - len(starts))
    block = block.reshape((1,) * (buffer.ndim - block.ndim) + block.shape)
    return lax.dynamic_update_slice(buffer, block, where)


def around(block, axis):
    return [block, fetch(block, **{axis: 1}), fetch(block, **{axis: 2}), fetch(block, **{axis: -1})]


def rows_over_pairs(rows, yh, z):
    high = z // HALF_Z
    pair = jnp.zeros((2,) + rows.shape, rows.dtype)
    pair = put(pair, rows, high)
    pair = put(pair, fetch(rows, z=HALF_Z), 1 - high)
    both = jnp.zeros((NY,) + pair.shape, rows.dtype)
    both = put(both, pair, yh)
    return put(both, fetch(pair, yh=1), 1 - yh)


def rows_over_z(both, z):
    line = jnp.zeros(both.shape[:2] + (HALF_Z,) + both.shape[2:], both.dtype)
    for hop, got in enumerate(around(both, "z")):
        line = lax.dynamic_update_slice(
            line, got[:, :, None], (0, 0, (z + hop) % HALF_Z, 0, 0)
        )
    return line.reshape((NY, NZ) + both.shape[2:])


def rows_over_x(line, x):
    whole = jnp.zeros((NY, NX) + line.shape[1:], line.dtype)
    for hop, got in enumerate(around(line, "x")):
        whole = lax.dynamic_update_slice(whole, got[:, None], (0, (x + hop) % NX, 0, 0, 0))
    return whole


STEP = 256


def place_a(weight, piece, spot_ref, first, hop):
    yh, x, z = spot_ref[0], spot_ref[1], spot_ref[2]
    depth = piece.shape[1]

    @pl.loop(0, piece.shape[0])
    def _(i):
        at_y = (yh + (i // 2) % 2) % NY
        at_x = (x + first + i // 4) % NX
        at_z = (z + (hop + NZ) + (i % 2) * HALF_Z) % NZ
        shard = ((at_y * NX + at_x) * 2 + at_z // HALF_Z) * 2 + at_z % 2
        weight[pl.ds(pl.multiple_of(shard * depth, depth), depth), :] = piece[i]


def product_a(grad_ref, rows, weight, tile):
    columns = []
    for part in range(NY * NX * 2):
        start = part * 2 * LANES + tile * LANES
        columns.append(grad_ref[rows, pl.ds(pl.multiple_of(start, LANES), LANES)])
    return jnp.dot(
        jnp.concatenate(columns, 1), weight[...], preferred_element_type=jnp.float32
    )


def place_b(weight, piece, spot_ref, first):
    yh, z = spot_ref[0], spot_ref[2]
    depth = piece.shape[1]

    @pl.loop(0, piece.shape[0])
    def _(i):
        hop = first + i // 4
        at_y = (yh + (i // 2) % 2) % NY
        at_z = (z + hop + (hop // 3 + i % 2) * HALF_Z) % NZ
        shard = at_y * NZ + at_z
        weight[pl.ds(pl.multiple_of(shard * depth, depth), depth), :] = piece[i]


def product_b(grad_ref, rows, weight, at_x):
    half = weight.shape[0] // NY
    columns = []
    for at_y in range(NY):
        start = (at_y * NX + at_x) * half
        columns.append(grad_ref[rows, pl.ds(pl.multiple_of(start, half), half)])
    return jnp.dot(
        jnp.concatenate(columns, 1), weight[...], preferred_element_type=jnp.float32
    )


def over_rows(grad_ref, body):
    @pl.loop(0, grad_ref.shape[0] // STEP)
    def _(i):
        body(pl.ds(pl.multiple_of(i * STEP, STEP), STEP))


def near_part(
    spot_ref, grad_ref, own_a, up_a, down_a, own_b, up_b, down_b, sum_a, sum_b, weight_a, weight_b
):
    x, z = spot_ref[1], spot_ref[2]
    place_a(weight_a, own_a, spot_ref, 0, 0)

    @pl.when(z % 2 == 0)
    def _():
        place_a(weight_a, up_a, spot_ref, 0, 1)

    @pl.when(z % 2 == 1)
    def _():
        place_a(weight_a, down_a, spot_ref, 0, -1)

    def first(rows):
        sum_a[rows, :] = product_a(grad_ref, rows, weight_a, z // 2 % 2)

    over_rows(grad_ref, first)
    for piece, hop in ((own_b, 0), (up_b, 1), (down_b, NX - 1)):
        place_b(weight_b, piece, spot_ref, 0)

        def add(rows):
            part = product_b(grad_ref, rows, weight_b, (x + hop) % NX)
            sum_b[rows, :] = part if hop == 0 else sum_b[rows, :] + part

        over_rows(grad_ref, add)


def far_part(
    spot_ref, grad_ref, sum_a, sum_b, up_a, down_a, far_up_a, far_down_a, far_up_b, far_down_b,
    out_ref, weight_a, weight_b,
):
    x, z = spot_ref[1], spot_ref[2]
    width = weight_a.shape[1]

    @pl.when(z % 2 == 1)
    def _():
        place_a(weight_a, up_a, spot_ref, 0, 1)

    @pl.when(z % 2 == 0)
    def _():
        place_a(weight_a, down_a, spot_ref, 0, -1)

    place_a(weight_a, far_up_a, spot_ref, 0, 2)
    place_a(weight_a, far_down_a, spot_ref, 2, -2)
    place_b(weight_b, far_up_b, spot_ref, 0)
    place_b(weight_b, far_down_b, spot_ref, 2)

    def last(rows):
        part = product_a(grad_ref, rows, weight_a, 1 - z // 2 % 2)
        out_ref[rows, :width] = (sum_a[rows, :] + part).astype(out_ref.dtype)
        part = product_b(grad_ref, rows, weight_b, (x + 2) % NX)
        out_ref[rows, width:] = (sum_b[rows, :] + part).astype(out_ref.dtype)

    over_rows(grad_ref, last)


def on_core(kernel, out_shape, spot, operands, scratch=(), flops=0):
    moved = sum(x.size * x.dtype.itemsize for x in operands)
    return pl.pallas_call(
        kernel,
        out_shape=out_shape,
        in_specs=[pl.BlockSpec(memory_space=pltpu.SMEM)]
        + [pl.BlockSpec(memory_space=pltpu.VMEM)] * len(operands),
        out_specs=jax.tree.map(lambda _: pl.BlockSpec(memory_space=pltpu.VMEM), out_shape),
        scratch_shapes=list(scratch),
        compiler_params=pltpu.CompilerParams(vmem_limit_bytes=40 * 1024 * 1024),
        cost_estimate=pl.CostEstimate(flops=flops, bytes_accessed=moved, transcendentals=0),
    )(spot, *operands)


def on_device(attn_in, out_grad, o_weight, in_factor, out_factor, store):
    yh, x, z = (lax.axis_index(axis) for axis in DOCS)
    core = lax.axis_index("core")
    tok_rows = out_grad.shape[0]
    rank_size = in_factor.shape[1]
    count = tok_rows // LENGTH
    share = store.shape[1]
    half_width = o_weight.shape[0] // 2
    spot = jnp.stack([yh, x, z]).astype(jnp.int32)

    tie = lax.optimization_barrier

    shard = o_weight.T
    other = fetch(shard, z=HALF_Z)
    right = jnp.dot(out_grad, out_factor, preferred_element_type=jnp.float32)
    right, other = tie((right, other))

    pair = jnp.stack([shard, other], 0)
    both = jnp.concatenate([pair, fetch(pair, yh=1)], 0)
    left = jnp.dot(attn_in, in_factor, preferred_element_type=jnp.float32)
    partial_proj = jnp.einsum(
        "qlr,qls->qrs",
        left.reshape(count, LENGTH, rank_size),
        right.reshape(count, LENGTH, rank_size),
        precision=lax.Precision.HIGHEST,
    ).reshape(count * rank_size * rank_size // LANES, LANES)
    full_proj = partial_proj + fetch(partial_proj, core=1)
    full_proj, both = tie((full_proj, both))

    line_a = around(both[..., :half_width], "x")
    line_b = around(both[..., half_width:], "z")
    full_proj = full_proj + fetch(full_proj, yl=1)
    full_proj = full_proj.reshape(count, NL * NC, share // LANES, LANES)
    query_sq = jnp.sum(full_proj * full_proj, axis=(1, 2, 3))
    mine = lax.dynamic_index_in_dim(full_proj, lax.axis_index(DIM), 1, keepdims=False)
    unit_rows = mine * lax.rsqrt(query_sq + 1e-06)[:, None, None]
    rows = rows_over_pairs(unit_rows.reshape(count * share // LANES, LANES), yh, z)
    doc_sq = jnp.sum(store * store, axis=1)
    rows, line_a, line_b, doc_sq = tie((rows, line_a, line_b, doc_sq))
    line_a, line_b = jnp.concatenate(line_a, 0), jnp.concatenate(line_b, 0)

    up_a, down_a = fetch(line_a, z=1), fetch(line_a, z=-1)
    up_b, down_b = fetch(line_b, x=1), fetch(line_b, x=-1)
    all_rows = rows_over_x(rows_over_z(rows, z), x).reshape(NY * NX * NZ * count, share)
    partial_scores = lax.dot_general(
        all_rows,
        store,
        (((1,), (1,)), ((), ())),
        precision=lax.Precision.HIGH,
        preferred_element_type=jnp.float32,
    )
    partial_scores, up_a, down_a, up_b, down_b = tie((partial_scores, up_a, down_a, up_b, down_b))

    middle = line_a.shape[0] // 2
    far_a = [fetch(up_a[:middle], z=1), fetch(down_a[middle:], z=-1)]
    far_b = [fetch(up_b[:middle], x=1), fetch(down_b[middle:], x=-1)]
    half = partial_scores.shape[0] // NC
    norm_rows = jnp.broadcast_to(doc_sq[None, :], (8, doc_sq.shape[0]))
    kept = lax.dynamic_slice_in_dim(partial_scores, core * half, half, 0)
    given = lax.dynamic_slice_in_dim(partial_scores, (1 - core) * half, half, 0)
    kept = jnp.concatenate([kept, norm_rows], 0)
    given = jnp.concatenate([given, norm_rows], 0)
    kept = kept + fetch(given, core=1)
    kept = kept + fetch(kept, yl=1)
    kept = kept[:half] * (float(rank_size) * lax.rsqrt(kept[half] + 1e-06))[None, :]
    other = fetch(kept, core=1)
    scores = jnp.concatenate(
        [jnp.where(core == 0, kept, other), jnp.where(core == 0, other, kept)], 0
    )
    weights = [
        pltpu.VMEM((out_grad.shape[1] // 2, half_width), out_grad.dtype),
        pltpu.VMEM((out_grad.shape[1] // 4, half_width), out_grad.dtype),
    ]
    sums = jax.ShapeDtypeStruct((tok_rows, half_width), jnp.float32)
    flops = 2 * tok_rows * out_grad.shape[1] * half_width
    sum_a, sum_b = on_core(
        near_part,
        (sums, sums),
        spot,
        [out_grad, line_a, up_a, down_a, line_b, up_b, down_b],
        weights,
        flops * 5 // 4,
    )
    in_cotangent = on_core(
        far_part,
        jax.ShapeDtypeStruct((tok_rows, 2 * half_width), out_grad.dtype),
        spot,
        [out_grad, sum_a, sum_b, up_a, down_a] + far_a + far_b,
        weights,
        flops * 3 // 4,
    )
    return (in_cotangent, scores)


def solution(mesh):
    mesh = Mesh(mesh.devices.reshape(NY, NX, NZ, NL, NC), NAMES)
    placed = (
        P(DOCS, DIM),
        P(DOCS, None),
        P(DIM, DOCS),
        P(DIM, None),
        P(),
        P(DOCS, DIM),
    )
    return jax.shard_map(
        on_device,
        mesh=mesh,
        in_specs=placed,
        out_specs=(P(DOCS, DIM), P(None, DOCS)),
        check_vma=False,
    )
```

```python
import functools

import jax
import jax.numpy as jnp
from jax import lax
from jax.experimental import pallas as pl
from jax.experimental.pallas import tpu as pltpu
from jax.sharding import Mesh
from jax.sharding import PartitionSpec as P

LENGTH = 256
NY, NX, NZ, NL, NC = 2, 4, 8, 2, 2
NAMES = ("yh", "x", "z", "yl", "core")
SIZES = dict(zip(NAMES, (NY, NX, NZ, NL, NC)))
DOCS = ("yh", "x", "z")
DIM = ("yl", "core")
LANES = 128
HALF_Z = NZ // 2


def fetch(value, **shift):
    ((axis, by),) = shift.items()
    size = SIZES[axis]
    return lax.ppermute(value, axis, [((to + by) % size, to) for to in range(size)])


def around(block, axis):
    return [block, fetch(block, **{axis: 1}), fetch(block, **{axis: 2}), fetch(block, **{axis: -1})]


STEP = 384


def build_lines(spot_ref, *refs):
    x, low = spot_ref[1], spot_ref[2] & (HALF_Z - 1)
    for hop in range(4):
        at_x, at_z = (x + hop) & (NX - 1), (low + hop) & (HALF_Z - 1)
        for at_y in range(NY):
            for high in range(2):
                refs[8 + at_y][at_x * 2 + high] = refs[hop][at_y, high]
                refs[10 + at_y][high * HALF_Z + at_z] = refs[4 + hop][at_y, high]


def place_a(weight, halves, bit):
    depth = halves[0].shape[1]
    for at_y, half in enumerate(halves):
        for block in range(half.shape[0]):
            start = ((at_y * half.shape[0] + block) * 2 + bit) * depth
            weight[pl.ds(pl.multiple_of(start, depth), depth), :] = half[block]


def place_b(weight, halves):
    depth = halves[0].shape[1]
    for index, half in enumerate(halves):
        for block in range(half.shape[0]):
            start = (index * half.shape[0] + block) * depth
            weight[start : start + depth, :] = half[block]


def product_a(grad_ref, rows, weight, tile):
    columns = []
    for part in range(NY * NX * 2):
        start = part * 2 * LANES + tile * LANES
        columns.append(grad_ref[rows, pl.ds(pl.multiple_of(start, LANES), LANES)])
    return jnp.dot(
        jnp.concatenate(columns, 1), weight[...], preferred_element_type=jnp.float32
    )


def product_b(grad_ref, rows, weight, at_xs):
    half = weight.shape[0] // (NY * len(at_xs))
    columns = []
    for at_x in at_xs:
        for at_y in range(NY):
            start = (at_y * NX + at_x) * half
            columns.append(grad_ref[rows, pl.ds(pl.multiple_of(start, half), half)])
    return jnp.dot(
        jnp.concatenate(columns, 1), weight[...], preferred_element_type=jnp.float32
    )


def over_rows(grad_ref, body):
    @pl.loop(0, grad_ref.shape[0] // STEP)
    def _(i):
        body(pl.ds(pl.multiple_of(i * STEP, STEP), STEP))


def near_part(spot_ref, grad_ref, *refs):
    own_a, up_a, down_a, own_b, up_b, down_b = (refs[i : i + 2] for i in range(0, 12, 2))
    sum_a, sum_b, weight_a, weight_b = refs[12:]
    x, z = spot_ref[1], spot_ref[2]
    bit = z & 1
    place_a(weight_a, own_a, bit)

    @pl.when(bit == 0)
    def _():
        place_a(weight_a, up_a, 1)

    @pl.when(bit == 1)
    def _():
        place_a(weight_a, down_a, 0)

    place_b(weight_b, (*own_b, *up_b, *down_b))

    def first(rows):
        sum_a[rows, :] = product_a(grad_ref, rows, weight_a, (z >> 1) & 1)
        at_xs = [(x + hop) & (NX - 1) for hop in (0, 1, 3)]
        sum_b[rows, :] = product_b(grad_ref, rows, weight_b, at_xs)

    over_rows(grad_ref, first)


def far_part(spot_ref, grad_ref, sum_a, sum_b, *refs):
    up_a, down_a, far_a, far_b = (refs[i : i + 2] for i in range(0, 8, 2))
    out_ref, weight_a, weight_b = refs[8:]
    x, z = spot_ref[1], spot_ref[2]
    width = weight_a.shape[1]
    bit = z & 1
    place_a(weight_a, far_a, bit)

    @pl.when(bit == 0)
    def _():
        place_a(weight_a, down_a, 1)

    @pl.when(bit == 1)
    def _():
        place_a(weight_a, up_a, 0)

    place_b(weight_b, far_b)

    def last(rows):
        part = product_a(grad_ref, rows, weight_a, 1 - ((z >> 1) & 1))
        out_ref[rows, :width] = (sum_a[rows, :] + part).astype(out_ref.dtype)
        part = product_b(grad_ref, rows, weight_b, [(x + 2) & (NX - 1)])
        out_ref[rows, width:] = (sum_b[rows, :] + part).astype(out_ref.dtype)

    over_rows(grad_ref, last)


def on_core(kernel, out_shape, spot, operands, scratch=(), flops=0):
    moved = sum(x.size * x.dtype.itemsize for x in operands)
    return pl.pallas_call(
        kernel,
        out_shape=out_shape,
        in_specs=[pl.BlockSpec(memory_space=pltpu.SMEM)]
        + [pl.BlockSpec(memory_space=pltpu.VMEM)] * len(operands),
        out_specs=jax.tree.map(lambda _: pl.BlockSpec(memory_space=pltpu.VMEM), out_shape),
        scratch_shapes=list(scratch),
        compiler_params=pltpu.CompilerParams(vmem_limit_bytes=40 * 1024 * 1024),
        cost_estimate=pl.CostEstimate(flops=flops, bytes_accessed=moved, transcendentals=0),
    )(spot, *operands)


def on_device(attn_in, out_grad, o_weight, in_factor, out_factor, store):
    yh, x, z = (lax.axis_index(axis) for axis in DOCS)
    core = lax.axis_index("core")
    tok_rows = out_grad.shape[0]
    rank_size = in_factor.shape[1]
    count = tok_rows // LENGTH
    share = store.shape[1]
    half_width = o_weight.shape[0] // 2
    spot = jnp.stack([yh, x, z]).astype(jnp.int32)

    tie = lax.optimization_barrier

    shard = o_weight.T
    other = fetch(shard, z=HALF_Z)
    right = jnp.dot(out_grad, out_factor, preferred_element_type=jnp.float32)
    right, other = tie((right, other))

    high = z // HALF_Z
    pair = jnp.stack([jnp.where(high == 0, shard, other), jnp.where(high == 0, other, shard)], 0)
    other = fetch(pair, yh=1)
    left = jnp.dot(attn_in, in_factor, preferred_element_type=jnp.float32)
    partial_proj = jnp.einsum(
        "qlr,qls->qrs",
        left.reshape(count, LENGTH, rank_size),
        right.reshape(count, LENGTH, rank_size),
        precision=lax.Precision.HIGHEST,
    ).reshape(count * rank_size * rank_size // LANES, LANES)
    full_proj = partial_proj + fetch(partial_proj, core=1)
    full_proj, other = tie((full_proj, other))

    full_proj = full_proj + fetch(full_proj, yl=1)
    full_proj = full_proj.reshape(count, NL * NC, share // LANES, LANES)
    query_sq = jnp.sum(full_proj * full_proj, axis=(1, 2, 3))
    mine = lax.dynamic_index_in_dim(full_proj, lax.axis_index(DIM), 1, keepdims=False)
    unit_rows = mine * lax.rsqrt(query_sq + 1e-06)[:, None, None]
    unit_rows = unit_rows.reshape(1, count * share // LANES, LANES)
    all_rows = lax.all_to_all(
        jnp.broadcast_to(unit_rows, (NY * NX * NZ,) + unit_rows.shape[1:]), DOCS, 0, 0
    ).reshape(NY * NX * NZ * count, share)

    both = jnp.stack([jnp.where(yh == 0, pair, other), jnp.where(yh == 0, other, pair)], 0)
    half_line = jax.ShapeDtypeStruct((NX * 2, shard.shape[0], half_width), shard.dtype)
    lines = on_core(
        build_lines,
        (half_line,) * 4,
        spot,
        around(both[..., :half_width], "x") + around(both[..., half_width:], "z"),
    )
    own_a, own_b = lines[:2], lines[2:]

    first = [
        fetch(own_b[0], x=1), fetch(own_b[1], x=-1), fetch(own_a[0], z=1), fetch(own_a[1], z=-1)
    ]
    second = [
        fetch(own_b[0], x=-1), fetch(own_b[1], x=1), fetch(own_a[0], z=-1), fetch(own_a[1], z=1)
    ]
    all_rows, *first = tie((all_rows, *first))
    far_b = [fetch(first[0], x=1), fetch(first[1], x=-1)]
    far_a = [fetch(first[2], z=1), fetch(first[3], z=-1)]

    doc_sq = jnp.sum(store * store, axis=1)
    partial_scores = lax.dot_general(
        all_rows,
        store,
        (((1,), (1,)), ((), ())),
        precision=lax.Precision.HIGH,
        preferred_element_type=jnp.float32,
    )
    half = partial_scores.shape[0] // NC
    norm_rows = jnp.broadcast_to(doc_sq[None, :], (8, doc_sq.shape[0]))
    kept = lax.dynamic_slice_in_dim(partial_scores, core * half, half, 0)
    given = lax.dynamic_slice_in_dim(partial_scores, (1 - core) * half, half, 0)
    kept = jnp.concatenate([kept, norm_rows], 0)
    given = jnp.concatenate([given, norm_rows], 0)
    kept = kept + fetch(given, core=1)
    kept, *second = tie((kept, *second))
    up_a, down_a = (first[2], second[3]), (second[2], first[3])
    up_b, down_b = (first[0], second[1]), (second[0], first[1])
    kept = kept + fetch(kept, yl=1)
    kept = kept[:half] * (float(rank_size) * lax.rsqrt(kept[half] + 1e-06))[None, :]
    other = fetch(kept, core=1)
    scores = jnp.concatenate(
        [jnp.where(core == 0, kept, other), jnp.where(core == 0, other, kept)], 0
    )

    def weights(*parts):
        depth = out_grad.shape[1]
        return [pltpu.VMEM((depth * part // 4, half_width), out_grad.dtype) for part in parts]

    sums = jax.ShapeDtypeStruct((tok_rows, half_width), jnp.float32)
    flops = 2 * tok_rows * out_grad.shape[1] * half_width
    sum_a, sum_b = on_core(
        near_part,
        (sums, sums),
        spot,
        [out_grad, *own_a, *up_a, *down_a, *own_b, *up_b, *down_b],
        weights(2, 3),
        flops * 5 // 4,
    )
    in_cotangent = on_core(
        far_part,
        jax.ShapeDtypeStruct((tok_rows, 2 * half_width), out_grad.dtype),
        spot,
        [out_grad, sum_a, sum_b, *up_a, *down_a, *far_a, *far_b],
        weights(2, 1),
        flops * 3 // 4,
    )
    return (in_cotangent, scores)


def solution(mesh):
    mesh = Mesh(mesh.devices.reshape(NY, NX, NZ, NL, NC), NAMES)
    placed = (
        P(DOCS, DIM),
        P(DOCS, None),
        P(DIM, DOCS),
        P(DIM, None),
        P(),
        P(DOCS, DIM),
    )
    return jax.shard_map(
        on_device,
        mesh=mesh,
        in_specs=placed,
        out_specs=(P(DOCS, DIM), P(None, DOCS)),
        check_vma=False,
    )
```

```python
import functools
import itertools

import jax
import jax.numpy as jnp
import numpy as np
from jax import lax
from jax.experimental import pallas as pl
from jax.experimental.pallas import tpu as pltpu
from jax.sharding import Mesh
from jax.sharding import PartitionSpec as P

LENGTH = 256
NY, NX, NZ, NL, NC = 2, 4, 8, 2, 2
NAMES = ("yh", "x", "z", "yl", "core")
SIZES = dict(zip(NAMES, (NY, NX, NZ, NL, NC)))
DOCS = ("yh", "x", "z")
DIM = ("yl", "core")
LANES = 128
HALF_Z = NZ // 2


def fetch(value, **shift):
    axes = tuple(shift)
    sizes = [SIZES[axis] for axis in axes]
    pairs = []
    for to in itertools.product(*map(range, sizes)):
        source = [(at + by) % size for at, by, size in zip(to, shift.values(), sizes)]
        pairs.append(tuple(int(np.ravel_multi_index(place, sizes)) for place in (source, to)))
    return lax.ppermute(value, axes, pairs)


def across(block):
    z, y = fetch(block, z=HALF_Z), fetch(block, yh=1)
    return [[block, z], [y, fetch(block, yh=1, z=HALF_Z)]]


def in_order(blocks, yh, high):
    (own, z), (y, both) = blocks

    def pair(first, second):
        return jnp.stack([jnp.where(high == 0, first, second), jnp.where(high == 0, second, first)])

    near, far = pair(own, z), pair(y, both)
    return jnp.stack([jnp.where(yh == 0, near, far), jnp.where(yh == 0, far, near)])


def along_x(block):
    return [block, fetch(block, x=1), fetch(block, x=2), fetch(block, x=-1)]


def along_z(block):
    far = [fetch(block[:1], z=2), fetch(block[1:], z=-2)]
    return [block, fetch(block, z=1), *far, fetch(block, z=-1)]


STEP = 384


def build_lines(spot_ref, *refs):
    x, low = spot_ref[1], spot_ref[2] & (HALF_Z - 1)
    from_x, from_z, out_a, out_b = refs[:4], refs[4:9], refs[9:11], refs[11:]
    for hop in range(4):
        at_x, at_z = (x + hop) & (NX - 1), (low + hop) & (HALF_Z - 1)
        for at_y in range(NY):
            for high in range(2):
                out_a[at_y][at_x * 2 + high] = from_x[hop][at_y, high]
                if hop == 2:
                    block = from_z[2 + at_y][0, high]
                else:
                    block = from_z[hop + hop // 3][at_y, high]
                out_b[at_y][high * HALF_Z + at_z] = block


def place_a(weight, halves, bit):
    depth = halves[0].shape[1]
    for at_y, half in enumerate(halves):
        for block in range(half.shape[0]):
            start = ((at_y * half.shape[0] + block) * 2 + bit) * depth
            weight[pl.ds(pl.multiple_of(start, depth), depth), :] = half[block]


def place_b(weight, halves):
    depth = halves[0].shape[1]
    for index, half in enumerate(halves):
        for block in range(half.shape[0]):
            start = (index * half.shape[0] + block) * depth
            weight[start : start + depth, :] = half[block]


def product_a(grad_ref, rows, weight, tile):
    columns = []
    for part in range(NY * NX * 2):
        start = part * 2 * LANES + tile * LANES
        columns.append(grad_ref[rows, pl.ds(pl.multiple_of(start, LANES), LANES)])
    return jnp.dot(
        jnp.concatenate(columns, 1), weight[...], preferred_element_type=jnp.float32
    )


def product_b(grad_ref, rows, weight, at_xs):
    half = weight.shape[0] // (NY * len(at_xs))
    columns = []
    for at_x in at_xs:
        for at_y in range(NY):
            start = (at_y * NX + at_x) * half
            columns.append(grad_ref[rows, pl.ds(pl.multiple_of(start, half), half)])
    return jnp.dot(
        jnp.concatenate(columns, 1), weight[...], preferred_element_type=jnp.float32
    )


def over_rows(grad_ref, body):
    @pl.loop(0, grad_ref.shape[0] // STEP)
    def _(i):
        body(pl.ds(pl.multiple_of(i * STEP, STEP), STEP))


def near_part(spot_ref, grad_ref, *refs):
    own_a, up_a, down_a, own_b, up_b, down_b = (refs[i : i + 2] for i in range(0, 12, 2))
    sum_a, sum_b, weight_a, weight_b = refs[12:]
    x, z = spot_ref[1], spot_ref[2]
    bit = z & 1
    place_a(weight_a, own_a, bit)

    @pl.when(bit == 0)
    def _():
        place_a(weight_a, up_a, 1)

    @pl.when(bit == 1)
    def _():
        place_a(weight_a, down_a, 0)

    place_b(weight_b, (*own_b, *up_b, *down_b))

    def first(rows):
        sum_a[rows, :] = product_a(grad_ref, rows, weight_a, (z >> 1) & 1)
        at_xs = [(x + hop) & (NX - 1) for hop in (0, 1, 3)]
        sum_b[rows, :] = product_b(grad_ref, rows, weight_b, at_xs)

    over_rows(grad_ref, first)


def far_part(spot_ref, grad_ref, sum_a, sum_b, *refs):
    up_a, down_a, far_a, far_b = (refs[i : i + 2] for i in range(0, 8, 2))
    out_ref, weight_a, weight_b = refs[8:]
    x, z = spot_ref[1], spot_ref[2]
    width = weight_a.shape[1]
    bit = z & 1
    place_a(weight_a, far_a, bit)

    @pl.when(bit == 0)
    def _():
        place_a(weight_a, down_a, 1)

    @pl.when(bit == 1)
    def _():
        place_a(weight_a, up_a, 0)

    place_b(weight_b, far_b)

    def last(rows):
        part = product_a(grad_ref, rows, weight_a, 1 - ((z >> 1) & 1))
        out_ref[rows, :width] = (sum_a[rows, :] + part).astype(out_ref.dtype)
        part = product_b(grad_ref, rows, weight_b, [(x + 2) & (NX - 1)])
        out_ref[rows, width:] = (sum_b[rows, :] + part).astype(out_ref.dtype)

    over_rows(grad_ref, last)


def on_core(kernel, out_shape, spot, operands, scratch=(), flops=0):
    moved = sum(x.size * x.dtype.itemsize for x in operands)
    return pl.pallas_call(
        kernel,
        out_shape=out_shape,
        in_specs=[pl.BlockSpec(memory_space=pltpu.SMEM)]
        + [pl.BlockSpec(memory_space=pltpu.VMEM)] * len(operands),
        out_specs=jax.tree.map(lambda _: pl.BlockSpec(memory_space=pltpu.VMEM), out_shape),
        scratch_shapes=list(scratch),
        compiler_params=pltpu.CompilerParams(vmem_limit_bytes=40 * 1024 * 1024),
        cost_estimate=pl.CostEstimate(flops=flops, bytes_accessed=moved, transcendentals=0),
    )(spot, *operands)


def on_device(attn_in, out_grad, o_weight, in_factor, out_factor, store):
    yh, x, z = (lax.axis_index(axis) for axis in DOCS)
    core = lax.axis_index("core")
    tok_rows = out_grad.shape[0]
    rank_size = in_factor.shape[1]
    count = tok_rows // LENGTH
    share = store.shape[1]
    half_width = o_weight.shape[0] // 2
    spot = jnp.stack([yh, x, z]).astype(jnp.int32)

    tie = lax.optimization_barrier

    high, low = z // HALF_Z, z % HALF_Z
    four = across(o_weight.T)
    right = jnp.dot(out_grad, out_factor, preferred_element_type=jnp.float32)
    left = jnp.dot(attn_in, in_factor, preferred_element_type=jnp.float32)
    partial_proj = jnp.einsum(
        "qlr,qls->qrs",
        left.reshape(count, LENGTH, rank_size),
        right.reshape(count, LENGTH, rank_size),
        precision=lax.Precision.HIGHEST,
    ).reshape(count * rank_size * rank_size // LANES, LANES)
    partial_proj, four = tie((partial_proj, four))

    both = in_order(four, yh, high)
    from_x = along_x(both[..., :half_width])
    from_z = along_z(both[..., half_width:])

    full_proj = partial_proj + fetch(partial_proj, core=1)
    full_proj = full_proj + fetch(full_proj, yl=1)
    full_proj = full_proj.reshape(count, NL * NC, share // LANES, LANES)
    query_sq = jnp.sum(full_proj * full_proj, axis=(1, 2, 3))
    mine = lax.dynamic_index_in_dim(full_proj, lax.axis_index(DIM), 1, keepdims=False)
    unit_rows = mine * lax.rsqrt(query_sq + 1e-06)[:, None, None]
    rows = in_order(across(unit_rows.reshape(count * share // LANES, LANES)), yh, high)
    rows, from_x, from_z = tie((rows, from_x, from_z))

    row_line = jnp.zeros((NY, 2, HALF_Z) + rows.shape[2:], rows.dtype)
    for hop, got in ((0, rows), (1, fetch(rows, z=1)), (2, fetch(rows, z=2)), (3, fetch(rows, z=-1))):
        where = (0, 0, (low + hop) % HALF_Z, 0, 0)
        row_line = lax.dynamic_update_slice(row_line, got[:, :, None], where)
    row_line = row_line.reshape((NY, NZ) + rows.shape[2:])

    half_line = jax.ShapeDtypeStruct((NX * 2, o_weight.shape[1], half_width), o_weight.dtype)
    lines = on_core(build_lines, (half_line,) * 4, spot, from_x + from_z)
    own_a, own_b = lines[:2], lines[2:]

    all_rows = jnp.zeros((NY, NX) + row_line.shape[1:], rows.dtype)
    for hop, got in enumerate(along_x(row_line)):
        where = (0, (x + hop) % NX, 0, 0, 0)
        all_rows = lax.dynamic_update_slice(all_rows, got[:, None], where)
    all_rows = all_rows.reshape(NY * NX * NZ * count, share)

    first = [
        fetch(own_b[0], x=1), fetch(own_b[1], x=-1), fetch(own_a[0], z=1), fetch(own_a[1], z=-1)
    ]
    second = [
        fetch(own_b[0], x=-1), fetch(own_b[1], x=1), fetch(own_a[0], z=-1), fetch(own_a[1], z=1)
    ]

    doc_sq = jnp.sum(store * store, axis=1)
    partial_scores = lax.dot_general(
        all_rows,
        store,
        (((1,), (1,)), ((), ())),
        precision=lax.Precision.HIGH,
        preferred_element_type=jnp.float32,
    )
    partial_scores, *first = tie((partial_scores, *first))
    far_b = [fetch(first[0], x=1), fetch(first[1], x=-1)]
    far_a = [fetch(first[2], z=1), fetch(first[3], z=-1)]
    half = partial_scores.shape[0] // NC
    norm_rows = jnp.broadcast_to(doc_sq[None, :], (8, doc_sq.shape[0]))
    kept = lax.dynamic_slice_in_dim(partial_scores, core * half, half, 0)
    given = lax.dynamic_slice_in_dim(partial_scores, (1 - core) * half, half, 0)
    kept = jnp.concatenate([kept, norm_rows], 0)
    given = jnp.concatenate([given, norm_rows], 0)
    kept = kept + fetch(given, core=1)
    kept, *second = tie((kept, *second))
    up_a, down_a = (first[2], second[3]), (second[2], first[3])
    up_b, down_b = (first[0], second[1]), (second[0], first[1])
    kept = kept + fetch(kept, yl=1)
    kept = kept[:half] * (float(rank_size) * lax.rsqrt(kept[half] + 1e-06))[None, :]
    other = fetch(kept, core=1)
    scores = jnp.concatenate(
        [jnp.where(core == 0, kept, other), jnp.where(core == 0, other, kept)], 0
    )

    def weights(*parts):
        depth = out_grad.shape[1]
        return [pltpu.VMEM((depth * part // 4, half_width), out_grad.dtype) for part in parts]

    sums = jax.ShapeDtypeStruct((tok_rows, half_width), jnp.float32)
    flops = 2 * tok_rows * out_grad.shape[1] * half_width
    sum_a, sum_b = on_core(
        near_part,
        (sums, sums),
        spot,
        [out_grad, *own_a, *up_a, *down_a, *own_b, *up_b, *down_b],
        weights(2, 3),
        flops * 5 // 4,
    )
    in_cotangent = on_core(
        far_part,
        jax.ShapeDtypeStruct((tok_rows, 2 * half_width), out_grad.dtype),
        spot,
        [out_grad, sum_a, sum_b, *up_a, *down_a, *far_a, *far_b],
        weights(2, 1),
        flops * 3 // 4,
    )
    return (in_cotangent, scores)


def solution(mesh):
    mesh = Mesh(mesh.devices.reshape(NY, NX, NZ, NL, NC), NAMES)
    placed = (
        P(DOCS, DIM),
        P(DOCS, None),
        P(DIM, DOCS),
        P(DIM, None),
        P(),
        P(DOCS, DIM),
    )
    return jax.shard_map(
        on_device,
        mesh=mesh,
        in_specs=placed,
        out_specs=(P(DOCS, DIM), P(None, DOCS)),
        check_vma=False,
    )
```

```python
import functools

import jax
import jax.numpy as jnp
from jax import lax
from jax.experimental import pallas as pl
from jax.experimental.pallas import tpu as pltpu
from jax.sharding import Mesh
from jax.sharding import PartitionSpec as P

LENGTH = 256
NY, NX, NZ, NL, NC = 2, 4, 8, 2, 2
NAMES = ("yh", "x", "z", "yl", "core")
SIZES = dict(zip(NAMES, (NY, NX, NZ, NL, NC)))
DOCS = ("yh", "x", "z")
DIM = ("yl", "core")
LANES = 128
HALF_Z = NZ // 2


def fetch(value, **shift):
    ((axis, by),) = shift.items()
    size = SIZES[axis]
    return lax.ppermute(value, axis, [((to + by) % size, to) for to in range(size)])


def around(block, axis):
    return [block, fetch(block, **{axis: 1}), fetch(block, **{axis: 2}), fetch(block, **{axis: -1})]


STEP = 384


def build_lines(spot_ref, *refs):
    x, low = spot_ref[1], spot_ref[2] & (HALF_Z - 1)
    for hop in range(4):
        at_x, at_z = (x + hop) & (NX - 1), (low + hop) & (HALF_Z - 1)
        for at_y in range(NY):
            for high in range(2):
                refs[8 + at_y][at_x * 2 + high] = refs[hop][at_y, high]
                refs[10 + at_y][high * HALF_Z + at_z] = refs[4 + hop][at_y, high]


def place_a(weight, halves, bit):
    depth = halves[0].shape[1]
    for at_y, half in enumerate(halves):
        for block in range(half.shape[0]):
            start = ((at_y * half.shape[0] + block) * 2 + bit) * depth
            weight[pl.ds(pl.multiple_of(start, depth), depth), :] = half[block]


def place_b(weight, halves):
    depth = halves[0].shape[1]
    for index, half in enumerate(halves):
        for block in range(half.shape[0]):
            start = (index * half.shape[0] + block) * depth
            weight[start : start + depth, :] = half[block]


def product_a(grad_ref, rows, weight, tile):
    columns = []
    for part in range(NY * NX * 2):
        start = part * 2 * LANES + tile * LANES
        columns.append(grad_ref[rows, pl.ds(pl.multiple_of(start, LANES), LANES)])
    return jnp.dot(
        jnp.concatenate(columns, 1), weight[...], preferred_element_type=jnp.float32
    )


def product_b(grad_ref, rows, weight, at_xs):
    half = weight.shape[0] // (NY * len(at_xs))
    columns = []
    for at_x in at_xs:
        for at_y in range(NY):
            start = (at_y * NX + at_x) * half
            columns.append(grad_ref[rows, pl.ds(pl.multiple_of(start, half), half)])
    return jnp.dot(
        jnp.concatenate(columns, 1), weight[...], preferred_element_type=jnp.float32
    )


def over_rows(grad_ref, body):
    @pl.loop(0, grad_ref.shape[0] // STEP)
    def _(i):
        body(pl.ds(pl.multiple_of(i * STEP, STEP), STEP))


def near_part(spot_ref, grad_ref, *refs):
    own_a, up_a, down_a, own_b, up_b, down_b = (refs[i : i + 2] for i in range(0, 12, 2))
    sum_a, sum_b, weight_a, weight_b = refs[12:]
    x, z = spot_ref[1], spot_ref[2]
    bit = z & 1
    place_a(weight_a, own_a, bit)

    @pl.when(bit == 0)
    def _():
        place_a(weight_a, up_a, 1)

    @pl.when(bit == 1)
    def _():
        place_a(weight_a, down_a, 0)

    place_b(weight_b, (*own_b, *up_b, *down_b))

    def first(rows):
        sum_a[rows, :] = product_a(grad_ref, rows, weight_a, (z >> 1) & 1)
        at_xs = [(x + hop) & (NX - 1) for hop in (0, 1, 3)]
        sum_b[rows, :] = product_b(grad_ref, rows, weight_b, at_xs)

    over_rows(grad_ref, first)


def far_part(spot_ref, grad_ref, sum_a, sum_b, *refs):
    up_a, down_a, far_a, far_b = (refs[i : i + 2] for i in range(0, 8, 2))
    out_ref, weight_a, weight_b = refs[8:]
    x, z = spot_ref[1], spot_ref[2]
    width = weight_a.shape[1]
    bit = z & 1
    place_a(weight_a, far_a, bit)

    @pl.when(bit == 0)
    def _():
        place_a(weight_a, down_a, 1)

    @pl.when(bit == 1)
    def _():
        place_a(weight_a, up_a, 0)

    place_b(weight_b, far_b)

    def last(rows):
        part = product_a(grad_ref, rows, weight_a, 1 - ((z >> 1) & 1))
        out_ref[rows, :width] = (sum_a[rows, :] + part).astype(out_ref.dtype)
        part = product_b(grad_ref, rows, weight_b, [(x + 2) & (NX - 1)])
        out_ref[rows, width:] = (sum_b[rows, :] + part).astype(out_ref.dtype)

    over_rows(grad_ref, last)


def on_core(kernel, out_shape, spot, operands, scratch=(), flops=0):
    moved = sum(x.size * x.dtype.itemsize for x in operands)
    return pl.pallas_call(
        kernel,
        out_shape=out_shape,
        in_specs=[pl.BlockSpec(memory_space=pltpu.SMEM)]
        + [pl.BlockSpec(memory_space=pltpu.VMEM)] * len(operands),
        out_specs=jax.tree.map(lambda _: pl.BlockSpec(memory_space=pltpu.VMEM), out_shape),
        scratch_shapes=list(scratch),
        compiler_params=pltpu.CompilerParams(vmem_limit_bytes=40 * 1024 * 1024),
        cost_estimate=pl.CostEstimate(flops=flops, bytes_accessed=moved, transcendentals=0),
    )(spot, *operands)


def on_device(attn_in, out_grad, o_weight, in_factor, out_factor, store):
    yh, x, z = (lax.axis_index(axis) for axis in DOCS)
    core = lax.axis_index("core")
    tok_rows = out_grad.shape[0]
    rank_size = in_factor.shape[1]
    count = tok_rows // LENGTH
    share = store.shape[1]
    half_width = o_weight.shape[0] // 2
    spot = jnp.stack([yh, x, z]).astype(jnp.int32)

    tie = lax.optimization_barrier

    shard = o_weight.T
    other = fetch(shard, z=HALF_Z)
    right = jnp.dot(out_grad, out_factor, preferred_element_type=jnp.float32)
    right, other = tie((right, other))

    high = z // HALF_Z
    pair = jnp.stack([jnp.where(high == 0, shard, other), jnp.where(high == 0, other, shard)], 0)
    other = fetch(pair, yh=1)
    left = jnp.dot(attn_in, in_factor, preferred_element_type=jnp.float32)
    partial_proj = jnp.einsum(
        "qlr,qls->qrs",
        left.reshape(count, LENGTH, rank_size),
        right.reshape(count, LENGTH, rank_size),
        precision=lax.Precision.HIGHEST,
    ).reshape(count * rank_size * rank_size // LANES, LANES)
    full_proj = partial_proj + fetch(partial_proj, core=1)
    full_proj, other = tie((full_proj, other))

    full_proj = full_proj + fetch(full_proj, yl=1)
    full_proj = full_proj.reshape(count, NL * NC, share // LANES, LANES)
    query_sq = jnp.sum(full_proj * full_proj, axis=(1, 2, 3))
    mine = lax.dynamic_index_in_dim(full_proj, lax.axis_index(DIM), 1, keepdims=False)
    unit_rows = mine * lax.rsqrt(query_sq + 1e-06)[:, None, None]
    unit_rows = unit_rows.reshape(1, count * share // LANES, LANES)
    all_rows = lax.all_to_all(
        jnp.broadcast_to(unit_rows, (NY * NX * NZ,) + unit_rows.shape[1:]), DOCS, 0, 0
    ).reshape(NY * NX * NZ * count, share)

    both = jnp.stack([jnp.where(yh == 0, pair, other), jnp.where(yh == 0, other, pair)], 0)
    half_line = jax.ShapeDtypeStruct((NX * 2, shard.shape[0], half_width), shard.dtype)
    lines = on_core(
        build_lines,
        (half_line,) * 4,
        spot,
        around(both[..., :half_width], "x") + around(both[..., half_width:], "z"),
        flops=10000000000,
    )
    own_a, own_b = lines[:2], lines[2:]

    first = [
        fetch(own_b[0], x=1), fetch(own_b[1], x=-1), fetch(own_a[0], z=1), fetch(own_a[1], z=-1)
    ]
    second = [
        fetch(own_b[0], x=-1), fetch(own_b[1], x=1), fetch(own_a[0], z=-1), fetch(own_a[1], z=1)
    ]
    all_rows, *first = tie((all_rows, *first))
    far_b = [fetch(first[0], x=1), fetch(first[1], x=-1)]
    far_a = [fetch(first[2], z=1), fetch(first[3], z=-1)]

    doc_sq = jnp.sum(store * store, axis=1)
    partial_scores = lax.dot_general(
        all_rows,
        store,
        (((1,), (1,)), ((), ())),
        precision=lax.Precision.HIGH,
        preferred_element_type=jnp.float32,
    )
    half = partial_scores.shape[0] // NC
    norm_rows = jnp.broadcast_to(doc_sq[None, :], (8, doc_sq.shape[0]))
    kept = lax.dynamic_slice_in_dim(partial_scores, core * half, half, 0)
    given = lax.dynamic_slice_in_dim(partial_scores, (1 - core) * half, half, 0)
    kept = jnp.concatenate([kept, norm_rows], 0)
    given = jnp.concatenate([given, norm_rows], 0)
    kept = kept + fetch(given, core=1)
    kept, *second = tie((kept, *second))
    up_a, down_a = (first[2], second[3]), (second[2], first[3])
    up_b, down_b = (first[0], second[1]), (second[0], first[1])
    kept = kept + fetch(kept, yl=1)
    kept = kept[:half] * (float(rank_size) * lax.rsqrt(kept[half] + 1e-06))[None, :]
    other = fetch(kept, core=1)
    scores = jnp.concatenate(
        [jnp.where(core == 0, kept, other), jnp.where(core == 0, other, kept)], 0
    )

    def weights(*parts):
        depth = out_grad.shape[1]
        return [pltpu.VMEM((depth * part // 4, half_width), out_grad.dtype) for part in parts]

    sums = jax.ShapeDtypeStruct((tok_rows, half_width), jnp.float32)
    flops = 2 * tok_rows * out_grad.shape[1] * half_width
    sum_a, sum_b = on_core(
        near_part,
        (sums, sums),
        spot,
        [out_grad, *own_a, *up_a, *down_a, *own_b, *up_b, *down_b],
        weights(2, 3),
        flops * 5 // 4,
    )
    in_cotangent = on_core(
        far_part,
        jax.ShapeDtypeStruct((tok_rows, 2 * half_width), out_grad.dtype),
        spot,
        [out_grad, sum_a, sum_b, *up_a, *down_a, *far_a, *far_b],
        weights(2, 1),
        flops * 3 // 4,
    )
    return (in_cotangent, scores)


def solution(mesh):
    mesh = Mesh(mesh.devices.reshape(NY, NX, NZ, NL, NC), NAMES)
    placed = (
        P(DOCS, DIM),
        P(DOCS, None),
        P(DIM, DOCS),
        P(DIM, None),
        P(),
        P(DOCS, DIM),
    )
    return jax.shard_map(
        on_device,
        mesh=mesh,
        in_specs=placed,
        out_specs=(P(DOCS, DIM), P(None, DOCS)),
        check_vma=False,
    )
```

```python
import functools

import jax
import jax.numpy as jnp
from jax import lax
from jax.experimental import pallas as pl
from jax.experimental.pallas import tpu as pltpu
from jax.sharding import Mesh
from jax.sharding import PartitionSpec as P

LENGTH = 256
NY, NX, NZ, NL, NC = 2, 4, 8, 2, 2
NAMES = ("yh", "x", "z", "yl", "core")
SIZES = dict(zip(NAMES, (NY, NX, NZ, NL, NC)))
DOCS = ("yh", "x", "z")
DIM = ("yl", "core")
LANES = 128
HALF_Z = NZ // 2


def fetch(value, **shift):
    ((axis, by),) = shift.items()
    size = SIZES[axis]
    return lax.ppermute(value, axis, [((to + by) % size, to) for to in range(size)])


def around(block, axis):
    return [block, fetch(block, **{axis: 1}), fetch(block, **{axis: 2}), fetch(block, **{axis: -1})]


STEP = 384


def build_lines(spot_ref, *refs):
    x, low = spot_ref[1], spot_ref[2] & (HALF_Z - 1)
    for hop in range(4):
        at_x, at_z = (x + hop) & (NX - 1), (low + hop) & (HALF_Z - 1)
        for at_y in range(NY):
            for high in range(2):
                refs[8 + at_y][at_x * 2 + high] = refs[hop][at_y, high]
                refs[10 + at_y][high * HALF_Z + at_z] = refs[4 + hop][at_y, high]


def place_a(weight, halves, bit):
    depth = halves[0].shape[1]
    for at_y, half in enumerate(halves):
        for block in range(half.shape[0]):
            start = ((at_y * half.shape[0] + block) * 2 + bit) * depth
            weight[pl.ds(pl.multiple_of(start, depth), depth), :] = half[block]


def place_b(weight, halves):
    depth = halves[0].shape[1]
    for index, half in enumerate(halves):
        for block in range(half.shape[0]):
            start = (index * half.shape[0] + block) * depth
            weight[start : start + depth, :] = half[block]


def product_a(grad_ref, rows, weight, tile):
    columns = []
    for part in range(NY * NX * 2):
        start = part * 2 * LANES + tile * LANES
        columns.append(grad_ref[rows, pl.ds(pl.multiple_of(start, LANES), LANES)])
    return jnp.dot(
        jnp.concatenate(columns, 1), weight[...], preferred_element_type=jnp.float32
    )


def product_b(grad_ref, rows, weight, at_xs):
    half = weight.shape[0] // (NY * len(at_xs))
    columns = []
    for at_x in at_xs:
        for at_y in range(NY):
            start = (at_y * NX + at_x) * half
            columns.append(grad_ref[rows, pl.ds(pl.multiple_of(start, half), half)])
    return jnp.dot(
        jnp.concatenate(columns, 1), weight[...], preferred_element_type=jnp.float32
    )


def over_rows(grad_ref, body):
    @pl.loop(0, grad_ref.shape[0] // STEP)
    def _(i):
        body(pl.ds(pl.multiple_of(i * STEP, STEP), STEP))


def near_part(spot_ref, grad_ref, *refs):
    own_a, up_a, down_a, own_b, up_b, down_b = (refs[i : i + 2] for i in range(0, 12, 2))
    sum_a, sum_b, weight_a, weight_b = refs[12:]
    x, z = spot_ref[1], spot_ref[2]
    bit = z & 1
    place_a(weight_a, own_a, bit)

    @pl.when(bit == 0)
    def _():
        place_a(weight_a, up_a, 1)

    @pl.when(bit == 1)
    def _():
        place_a(weight_a, down_a, 0)

    place_b(weight_b, (*own_b, *up_b, *down_b))

    def first(rows):
        sum_a[rows, :] = product_a(grad_ref, rows, weight_a, (z >> 1) & 1)
        at_xs = [(x + hop) & (NX - 1) for hop in (0, 1, 3)]
        sum_b[rows, :] = product_b(grad_ref, rows, weight_b, at_xs)

    over_rows(grad_ref, first)


def far_part(spot_ref, grad_ref, sum_a, sum_b, *refs):
    up_a, down_a, far_a, far_b = (refs[i : i + 2] for i in range(0, 8, 2))
    out_ref, weight_a, weight_b = refs[8:]
    x, z = spot_ref[1], spot_ref[2]
    width = weight_a.shape[1]
    bit = z & 1
    place_a(weight_a, far_a, bit)

    @pl.when(bit == 0)
    def _():
        place_a(weight_a, down_a, 1)

    @pl.when(bit == 1)
    def _():
        place_a(weight_a, up_a, 0)

    place_b(weight_b, far_b)

    def last(rows):
        part = product_a(grad_ref, rows, weight_a, 1 - ((z >> 1) & 1))
        out_ref[rows, :width] = (sum_a[rows, :] + part).astype(out_ref.dtype)
        part = product_b(grad_ref, rows, weight_b, [(x + 2) & (NX - 1)])
        out_ref[rows, width:] = (sum_b[rows, :] + part).astype(out_ref.dtype)

    over_rows(grad_ref, last)


def on_core(kernel, out_shape, spot, operands, scratch=(), flops=0):
    moved = sum(x.size * x.dtype.itemsize for x in operands)
    return pl.pallas_call(
        kernel,
        out_shape=out_shape,
        in_specs=[pl.BlockSpec(memory_space=pltpu.SMEM)]
        + [pl.BlockSpec(memory_space=pltpu.VMEM)] * len(operands),
        out_specs=jax.tree.map(lambda _: pl.BlockSpec(memory_space=pltpu.VMEM), out_shape),
        scratch_shapes=list(scratch),
        compiler_params=pltpu.CompilerParams(vmem_limit_bytes=40 * 1024 * 1024),
        cost_estimate=pl.CostEstimate(flops=flops, bytes_accessed=moved, transcendentals=0),
    )(spot, *operands)


def on_device(attn_in, out_grad, o_weight, in_factor, out_factor, store):
    yh, x, z = (lax.axis_index(axis) for axis in DOCS)
    core = lax.axis_index("core")
    tok_rows = out_grad.shape[0]
    rank_size = in_factor.shape[1]
    count = tok_rows // LENGTH
    share = store.shape[1]
    half_width = o_weight.shape[0] // 2
    spot = jnp.stack([yh, x, z]).astype(jnp.int32)

    tie = lax.optimization_barrier

    shard = o_weight.T
    other = fetch(shard, z=HALF_Z)
    right = jnp.dot(out_grad, out_factor, preferred_element_type=jnp.float32)
    right, other = tie((right, other))

    high = z // HALF_Z
    pair = jnp.stack([jnp.where(high == 0, shard, other), jnp.where(high == 0, other, shard)], 0)
    other = fetch(pair, yh=1)
    left = jnp.dot(attn_in, in_factor, preferred_element_type=jnp.float32)
    partial_proj = jnp.einsum(
        "qlr,qls->qrs",
        left.reshape(count, LENGTH, rank_size),
        right.reshape(count, LENGTH, rank_size),
        precision=lax.Precision.HIGHEST,
    ).reshape(count * rank_size * rank_size // LANES, LANES)
    full_proj = partial_proj + fetch(partial_proj, core=1)
    full_proj = full_proj + fetch(full_proj, yl=1)
    full_proj = full_proj.reshape(count, NL * NC, share // LANES, LANES)
    query_sq = jnp.sum(full_proj * full_proj, axis=(1, 2, 3))
    mine = lax.dynamic_index_in_dim(full_proj, lax.axis_index(DIM), 1, keepdims=False)
    unit_rows = mine * lax.rsqrt(query_sq + 1e-06)[:, None, None]
    unit_rows = (unit_rows * float(rank_size)).astype(jnp.float16)
    unit_rows = unit_rows.reshape(1, count * share // LANES, LANES)
    all_rows = lax.all_to_all(
        jnp.broadcast_to(unit_rows, (NY * NX * NZ,) + unit_rows.shape[1:]), DOCS, 0, 0
    )
    all_rows = all_rows.reshape(NY * NX * NZ * count, share).astype(jnp.float32)

    both = jnp.stack([jnp.where(yh == 0, pair, other), jnp.where(yh == 0, other, pair)], 0)
    half_line = jax.ShapeDtypeStruct((NX * 2, shard.shape[0], half_width), shard.dtype)
    lines = on_core(
        build_lines,
        (half_line,) * 4,
        spot,
        around(both[..., :half_width], "x") + around(both[..., half_width:], "z"),
        flops=10000000000,
    )
    own_a, own_b = lines[:2], lines[2:]

    first = [
        fetch(own_b[0], x=1), fetch(own_b[1], x=-1), fetch(own_a[0], z=1), fetch(own_a[1], z=-1)
    ]
    second = [
        fetch(own_b[0], x=-1), fetch(own_b[1], x=1), fetch(own_a[0], z=-1), fetch(own_a[1], z=1)
    ]
    all_rows, *first = tie((all_rows, *first))
    far_b = [fetch(first[0], x=1), fetch(first[1], x=-1)]
    far_a = [fetch(first[2], z=1), fetch(first[3], z=-1)]

    doc_sq = jnp.sum(store * store, axis=1)
    partial_scores = lax.dot_general(
        all_rows,
        store,
        (((1,), (1,)), ((), ())),
        precision=lax.Precision.HIGH,
        preferred_element_type=jnp.float32,
    )
    half = partial_scores.shape[0] // NC
    norm_rows = jnp.broadcast_to(doc_sq[None, :], (8, doc_sq.shape[0]))
    kept = lax.dynamic_slice_in_dim(partial_scores, core * half, half, 0)
    given = lax.dynamic_slice_in_dim(partial_scores, (1 - core) * half, half, 0)
    kept = jnp.concatenate([kept, norm_rows], 0)
    given = jnp.concatenate([given, norm_rows], 0)
    kept = kept + fetch(given, core=1)
    kept, *second = tie((kept, *second))
    up_a, down_a = (first[2], second[3]), (second[2], first[3])
    up_b, down_b = (first[0], second[1]), (second[0], first[1])
    kept = kept + fetch(kept, yl=1)
    kept = kept[:half] * lax.rsqrt(kept[half] + 1e-06)[None, :]
    other = fetch(kept, core=1)
    scores = jnp.concatenate(
        [jnp.where(core == 0, kept, other), jnp.where(core == 0, other, kept)], 0
    )

    def weights(*parts):
        depth = out_grad.shape[1]
        return [pltpu.VMEM((depth * part // 4, half_width), out_grad.dtype) for part in parts]

    sums = jax.ShapeDtypeStruct((tok_rows, half_width), jnp.float32)
    flops = 2 * tok_rows * out_grad.shape[1] * half_width
    sum_a, sum_b = on_core(
        near_part,
        (sums, sums),
        spot,
        [out_grad, *own_a, *up_a, *down_a, *own_b, *up_b, *down_b],
        weights(2, 3),
        flops * 5 // 4,
    )
    in_cotangent = on_core(
        far_part,
        jax.ShapeDtypeStruct((tok_rows, 2 * half_width), out_grad.dtype),
        spot,
        [out_grad, sum_a, sum_b, *up_a, *down_a, *far_a, *far_b],
        weights(2, 1),
        flops * 3 // 4,
    )
    return (in_cotangent, scores)


def solution(mesh):
    mesh = Mesh(mesh.devices.reshape(NY, NX, NZ, NL, NC), NAMES)
    placed = (
        P(DOCS, DIM),
        P(DOCS, None),
        P(DIM, DOCS),
        P(DIM, None),
        P(),
        P(DOCS, DIM),
    )
    return jax.shard_map(
        on_device,
        mesh=mesh,
        in_specs=placed,
        out_specs=(P(DOCS, DIM), P(None, DOCS)),
        check_vma=False,
    )
```

```python
import functools

import jax
import jax.numpy as jnp
from jax import lax
from jax.experimental import pallas as pl
from jax.experimental.pallas import tpu as pltpu
from jax.sharding import Mesh
from jax.sharding import PartitionSpec as P

LENGTH = 256
NY, NX, NZ, NL, NC = 2, 4, 8, 2, 2
NAMES = ("yh", "x", "z", "yl", "core")
SIZES = dict(zip(NAMES, (NY, NX, NZ, NL, NC)))
DOCS = ("yh", "x", "z")
DIM = ("yl", "core")
LANES = 128
HALF_Z = NZ // 2


def fetch(value, **shift):
    ((axis, by),) = shift.items()
    size = SIZES[axis]
    return lax.ppermute(value, axis, [((to + by) % size, to) for to in range(size)])


HOPS = (2, 1, 3, 0)


def around(block, axis):
    return [fetch(block, **{axis: hop}) for hop in (2, 1, -1)] + [block]


STEP = 384


def build_lines(spot_ref, *refs):
    x, low = spot_ref[1], spot_ref[2] & (HALF_Z - 1)
    for index, hop in enumerate(HOPS):
        at_x, at_z = (x + hop) & (NX - 1), (low + hop) & (HALF_Z - 1)
        for at_y in range(NY):
            for high in range(2):
                refs[8 + at_y][at_x * 2 + high] = refs[4 + index][at_y, high]
                refs[10 + at_y][high * HALF_Z + at_z] = refs[index][at_y, high]


def place_a(weight, halves, bit):
    depth = halves[0].shape[1]
    for index, half in enumerate(halves):
        for block in range(half.shape[0]):
            start = ((index * half.shape[0] + block) * 2 + bit) * depth
            weight[pl.ds(pl.multiple_of(start, depth), depth), :] = half[block]


def place_b(weight, halves):
    depth = halves[0].shape[1]
    for index, half in enumerate(halves):
        for block in range(half.shape[0]):
            start = (index * half.shape[0] + block) * depth
            weight[start : start + depth, :] = half[block]


def product_a(grad_ref, rows, weight, tile, at_ys):
    columns = []
    for at_y in at_ys:
        for part in range(NX * 2):
            start = (at_y * NX * 2 + part) * 2 * LANES + tile * LANES
            columns.append(grad_ref[rows, pl.ds(pl.multiple_of(start, LANES), LANES)])
    return jnp.dot(
        jnp.concatenate(columns, 1), weight[...], preferred_element_type=jnp.float32
    )


def product_b(grad_ref, rows, weight, places):
    half = weight.shape[0] // len(places)
    columns = []
    for at_y, at_x in places:
        start = (at_y * NX + (at_x & (NX - 1))) * half
        columns.append(grad_ref[rows, pl.ds(pl.multiple_of(start, half), half)])
    return jnp.dot(
        jnp.concatenate(columns, 1), weight[...], preferred_element_type=jnp.float32
    )


def over_rows(grad_ref, body):
    @pl.loop(0, grad_ref.shape[0] // STEP)
    def _(i):
        body(pl.ds(pl.multiple_of(i * STEP, STEP), STEP))


def first_part(spot_ref, grad_ref, *refs):
    own_a, (up_a, down_a), own_b, (up_b, down_b) = (refs[i : i + 2] for i in range(0, 8, 2))
    sum_a, sum_b, weight_a, weight_b = refs[8:]
    x, z = spot_ref[1], spot_ref[2]
    bit = z & 1

    @pl.when(bit == 0)
    def _():
        place_a(weight_a, own_a[:1], 0)
        place_a(weight_a, [up_a], 1)

    @pl.when(bit == 1)
    def _():
        place_a(weight_a, own_a[1:], 1)
        place_a(weight_a, [down_a], 0)

    place_b(weight_b, (*own_b, up_b, down_b))

    def body(rows):
        sum_a[rows, :] = product_a(grad_ref, rows, weight_a, (z >> 1) & 1, [bit])
        places = [(0, x), (1, x), (0, x + 1), (1, x + 3)]
        sum_b[rows, :] = product_b(grad_ref, rows, weight_b, places)

    over_rows(grad_ref, body)


def second_part(spot_ref, grad_ref, old_a, old_b, *refs):
    own_a, (up_a, down_a), (up_b, down_b) = (refs[i : i + 2] for i in range(0, 6, 2))
    sum_a, sum_b, weight_a, weight_b = refs[6:]
    x, z = spot_ref[1], spot_ref[2]
    bit = z & 1

    @pl.when(bit == 0)
    def _():
        place_a(weight_a, own_a[1:], 0)
        place_a(weight_a, [up_a], 1)

    @pl.when(bit == 1)
    def _():
        place_a(weight_a, own_a[:1], 1)
        place_a(weight_a, [down_a], 0)

    place_b(weight_b, (up_b, down_b))

    def body(rows):
        part = product_a(grad_ref, rows, weight_a, (z >> 1) & 1, [1 - bit])
        sum_a[rows, :] = old_a[rows, :] + part
        part = product_b(grad_ref, rows, weight_b, [(1, x + 1), (0, x + 3)])
        sum_b[rows, :] = old_b[rows, :] + part

    over_rows(grad_ref, body)


def far_part(spot_ref, grad_ref, sum_a, sum_b, *refs):
    up_a, down_a, far_a, far_b = (refs[i : i + 2] for i in range(0, 8, 2))
    out_ref, weight_a, weight_b = refs[8:]
    x, z = spot_ref[1], spot_ref[2]
    width = weight_a.shape[1]
    bit = z & 1
    place_a(weight_a, far_a, bit)

    @pl.when(bit == 0)
    def _():
        place_a(weight_a, down_a, 1)

    @pl.when(bit == 1)
    def _():
        place_a(weight_a, up_a, 0)

    place_b(weight_b, far_b)

    def body(rows):
        part = product_a(grad_ref, rows, weight_a, 1 - ((z >> 1) & 1), range(NY))
        out_ref[rows, :width] = (sum_a[rows, :] + part).astype(out_ref.dtype)
        part = product_b(grad_ref, rows, weight_b, [(0, x + 2), (1, x + 2)])
        out_ref[rows, width:] = (sum_b[rows, :] + part).astype(out_ref.dtype)

    over_rows(grad_ref, body)


def on_core(kernel, out_shape, spot, operands, scratch=(), flops=0):
    moved = sum(x.size * x.dtype.itemsize for x in operands)
    return pl.pallas_call(
        kernel,
        out_shape=out_shape,
        in_specs=[pl.BlockSpec(memory_space=pltpu.SMEM)]
        + [pl.BlockSpec(memory_space=pltpu.VMEM)] * len(operands),
        out_specs=jax.tree.map(lambda _: pl.BlockSpec(memory_space=pltpu.VMEM), out_shape),
        scratch_shapes=list(scratch),
        compiler_params=pltpu.CompilerParams(vmem_limit_bytes=40 * 1024 * 1024),
        cost_estimate=pl.CostEstimate(flops=flops, bytes_accessed=moved, transcendentals=0),
    )(spot, *operands)


def on_device(attn_in, out_grad, o_weight, in_factor, out_factor, store):
    yh, x, z = (lax.axis_index(axis) for axis in DOCS)
    core = lax.axis_index("core")
    tok_rows = out_grad.shape[0]
    rank_size = in_factor.shape[1]
    count = tok_rows // LENGTH
    share = store.shape[1]
    half_width = o_weight.shape[0] // 2
    spot = jnp.stack([yh, x, z]).astype(jnp.int32)

    tie = lax.optimization_barrier

    shard = o_weight.T
    other = fetch(shard, z=HALF_Z)
    right = jnp.dot(out_grad, out_factor, preferred_element_type=jnp.float32)
    right, other = tie((right, other))

    high = z // HALF_Z
    pair = jnp.stack([jnp.where(high == 0, shard, other), jnp.where(high == 0, other, shard)], 0)
    other = fetch(pair, yh=1)
    doc_sq = jnp.sum(store * store, axis=1)
    other, doc_sq = tie((other, doc_sq))
    left = jnp.dot(attn_in, in_factor, preferred_element_type=jnp.float32)
    partial_proj = jnp.einsum(
        "qlr,qls->qrs",
        left.reshape(count, LENGTH, rank_size),
        right.reshape(count, LENGTH, rank_size),
        precision=lax.Precision.HIGHEST,
    ).reshape(count * rank_size * rank_size // LANES, LANES)
    full_proj = partial_proj + fetch(partial_proj, core=1)
    full_proj = full_proj + fetch(full_proj, yl=1)
    full_proj = full_proj.reshape(count, NL * NC, share // LANES, LANES)
    query_sq = jnp.sum(full_proj * full_proj, axis=(1, 2, 3))
    mine = lax.dynamic_index_in_dim(full_proj, lax.axis_index(DIM), 1, keepdims=False)
    unit_rows = mine * lax.rsqrt(query_sq + 1e-06)[:, None, None]
    unit_rows = (unit_rows * float(rank_size)).astype(jnp.float16)
    unit_rows = unit_rows.reshape(1, count * share // LANES, LANES)
    all_rows = lax.all_to_all(
        jnp.broadcast_to(unit_rows, (NY * NX * NZ,) + unit_rows.shape[1:]), DOCS, 0, 0
    )

    both = jnp.stack([jnp.where(yh == 0, pair, other), jnp.where(yh == 0, other, pair)], 0)
    from_z = around(both[..., half_width:], "z")
    from_x = around(both[..., :half_width], "x")
    half_line = jax.ShapeDtypeStruct((NX * 2, shard.shape[0], half_width), shard.dtype)
    lines = on_core(
        build_lines,
        (half_line,) * 4,
        spot,
        from_z + from_x,
        flops=10000000000,
    )
    own_a, own_b = lines[:2], lines[2:]

    first = [
        fetch(own_b[0], x=1), fetch(own_b[1], x=-1), fetch(own_a[0], z=1), fetch(own_a[1], z=-1)
    ]
    second = [
        fetch(own_b[0], x=-1), fetch(own_b[1], x=1), fetch(own_a[0], z=-1), fetch(own_a[1], z=1)
    ]
    def weights(*parts):
        depth = out_grad.shape[1]
        return [pltpu.VMEM((depth * part // 4, half_width), out_grad.dtype) for part in parts]

    sums = jax.ShapeDtypeStruct((tok_rows, half_width), jnp.float32)
    flops = 2 * tok_rows * out_grad.shape[1] * half_width
    sum_a, sum_b = on_core(
        first_part,
        (sums, sums),
        spot,
        [out_grad, *own_a, *first[2:], *own_b, *first[:2]],
        weights(1, 2),
        4000000000,
    )
    all_rows, sum_a, sum_b = tie((all_rows, sum_a, sum_b))
    all_rows = all_rows.reshape(NY * NX * NZ * count, share).astype(jnp.float32)
    far_b = [fetch(first[0], x=1), fetch(first[1], x=-1)]
    far_a = [fetch(first[2], z=1), fetch(first[3], z=-1)]

    partial_scores = lax.dot_general(
        all_rows,
        store,
        (((1,), (1,)), ((), ())),
        precision=lax.Precision.HIGH,
        preferred_element_type=jnp.float32,
    )
    half = partial_scores.shape[0] // NC
    norm_rows = jnp.broadcast_to(doc_sq[None, :], (8, doc_sq.shape[0]))
    kept = lax.dynamic_slice_in_dim(partial_scores, core * half, half, 0)
    given = lax.dynamic_slice_in_dim(partial_scores, (1 - core) * half, half, 0)
    kept = jnp.concatenate([kept, norm_rows], 0)
    given = jnp.concatenate([given, norm_rows], 0)
    kept = kept + fetch(given, core=1)
    kept, *second = tie((kept, *second))
    up_a, down_a = (first[2], second[3]), (second[2], first[3])
    up_b, down_b = (first[0], second[1]), (second[0], first[1])
    kept = kept + fetch(kept, yl=1)
    kept = kept[:half] * lax.rsqrt(kept[half] + 1e-06)[None, :]
    other = fetch(kept, core=1)
    scores = jnp.concatenate(
        [jnp.where(core == 0, kept, other), jnp.where(core == 0, other, kept)], 0
    )

    sum_a, sum_b = on_core(
        second_part,
        (sums, sums),
        spot,
        [out_grad, sum_a, sum_b, *own_a, second[3], second[2], second[1], second[0]],
        weights(1, 1),
        flops // 2,
    )
    in_cotangent = on_core(
        far_part,
        jax.ShapeDtypeStruct((tok_rows, 2 * half_width), out_grad.dtype),
        spot,
        [out_grad, sum_a, sum_b, *up_a, *down_a, *far_a, *far_b],
        weights(2, 1),
        flops * 3 // 4,
    )
    return (in_cotangent, scores)


def solution(mesh):
    mesh = Mesh(mesh.devices.reshape(NY, NX, NZ, NL, NC), NAMES)
    placed = (
        P(DOCS, DIM),
        P(DOCS, None),
        P(DIM, DOCS),
        P(DIM, None),
        P(),
        P(DOCS, DIM),
    )
    return jax.shard_map(
        on_device,
        mesh=mesh,
        in_specs=placed,
        out_specs=(P(DOCS, DIM), P(None, DOCS)),
        check_vma=False,
    )
```

```python
import functools

import jax
import jax.numpy as jnp
from jax import lax
from jax.experimental import pallas as pl
from jax.experimental.pallas import tpu as pltpu
from jax.sharding import Mesh
from jax.sharding import PartitionSpec as P

LENGTH = 256
NY, NX, NZ, NL, NC = 2, 4, 8, 2, 2
NAMES = ("yh", "x", "z", "yl", "core")
SIZES = dict(zip(NAMES, (NY, NX, NZ, NL, NC)))
DOCS = ("yh", "x", "z")
DIM = ("yl", "core")
LANES = 128
HALF_Z = NZ // 2


def fetch(value, **shift):
    ((axis, by),) = shift.items()
    size = SIZES[axis]
    return lax.ppermute(value, axis, [((to + by) % size, to) for to in range(size)])


HOPS = (0, 3, 1, 2)


def around(block, axis):
    if axis == "z":
        pairs = [((to + (-2 if to % 2 else 2)) % NZ, to) for to in range(NZ)]
        far = lax.ppermute(block, axis, pairs)
    else:
        far = fetch(block, **{axis: 2})
    return [block, fetch(block, **{axis: -1}), fetch(block, **{axis: 1}), far]


STEP = 384


def build_lines(spot_ref, *refs):
    x, low = spot_ref[1], spot_ref[2] & (HALF_Z - 1)
    for index, hop in enumerate(HOPS):
        at_x, at_z = (x + hop) & (NX - 1), (low + hop) & (HALF_Z - 1)
        for at_y in range(NY):
            for high in range(2):
                refs[8 + at_y][at_x * 2 + high] = refs[index][at_y, high]
                refs[10 + at_y][high * HALF_Z + at_z] = refs[4 + index][at_y, high]


def place_a(weight, halves, bit):
    depth = halves[0].shape[1]
    for at_y, half in enumerate(halves):
        for block in range(half.shape[0]):
            start = ((at_y * half.shape[0] + block) * 2 + bit) * depth
            weight[pl.ds(pl.multiple_of(start, depth), depth), :] = half[block]


def place_b(weight, halves):
    depth = halves[0].shape[1]
    for index, half in enumerate(halves):
        for block in range(half.shape[0]):
            start = (index * half.shape[0] + block) * depth
            weight[start : start + depth, :] = half[block]


def product_a(grad_ref, rows, weight, tile):
    columns = []
    for part in range(NY * NX * 2):
        start = part * 2 * LANES + tile * LANES
        columns.append(grad_ref[rows, pl.ds(pl.multiple_of(start, LANES), LANES)])
    return jnp.dot(
        jnp.concatenate(columns, 1), weight[...], preferred_element_type=jnp.float32
    )


def product_b(grad_ref, rows, weight, at_xs):
    half = weight.shape[0] // (NY * len(at_xs))
    columns = []
    for at_x in at_xs:
        for at_y in range(NY):
            start = (at_y * NX + at_x) * half
            columns.append(grad_ref[rows, pl.ds(pl.multiple_of(start, half), half)])
    return jnp.dot(
        jnp.concatenate(columns, 1), weight[...], preferred_element_type=jnp.float32
    )


def over_rows(grad_ref, body):
    @pl.loop(0, grad_ref.shape[0] // STEP)
    def _(i):
        body(pl.ds(pl.multiple_of(i * STEP, STEP), STEP))


def near_part(spot_ref, grad_ref, *refs):
    own_a, up_a, down_a, own_b, up_b, down_b = (refs[i : i + 2] for i in range(0, 12, 2))
    sum_a, sum_b, weight_a, weight_b = refs[12:]
    x, z = spot_ref[1], spot_ref[2]
    bit = z & 1
    place_a(weight_a, own_a, bit)

    @pl.when(bit == 0)
    def _():
        place_a(weight_a, up_a, 1)

    @pl.when(bit == 1)
    def _():
        place_a(weight_a, down_a, 0)

    place_b(weight_b, (*own_b, *up_b, *down_b))

    def first(rows):
        sum_a[rows, :] = product_a(grad_ref, rows, weight_a, (z >> 1) & 1)
        at_xs = [(x + hop) & (NX - 1) for hop in (0, 1, 3)]
        sum_b[rows, :] = product_b(grad_ref, rows, weight_b, at_xs)

    over_rows(grad_ref, first)


def far_part(spot_ref, grad_ref, sum_a, sum_b, *refs):
    up_a, down_a, far_a, far_b = (refs[i : i + 2] for i in range(0, 8, 2))
    out_ref, weight_a, weight_b = refs[8:]
    x, z = spot_ref[1], spot_ref[2]
    width = weight_a.shape[1]
    bit = z & 1
    place_a(weight_a, far_a, bit)

    @pl.when(bit == 0)
    def _():
        place_a(weight_a, down_a, 1)

    @pl.when(bit == 1)
    def _():
        place_a(weight_a, up_a, 0)

    place_b(weight_b, far_b)

    def last(rows):
        part = product_a(grad_ref, rows, weight_a, 1 - ((z >> 1) & 1))
        out_ref[rows, :width] = (sum_a[rows, :] + part).astype(out_ref.dtype)
        part = product_b(grad_ref, rows, weight_b, [(x + 2) & (NX - 1)])
        out_ref[rows, width:] = (sum_b[rows, :] + part).astype(out_ref.dtype)

    over_rows(grad_ref, last)


def on_core(kernel, out_shape, spot, operands, scratch=(), flops=0):
    moved = sum(x.size * x.dtype.itemsize for x in operands)
    return pl.pallas_call(
        kernel,
        out_shape=out_shape,
        in_specs=[pl.BlockSpec(memory_space=pltpu.SMEM)]
        + [pl.BlockSpec(memory_space=pltpu.VMEM)] * len(operands),
        out_specs=jax.tree.map(lambda _: pl.BlockSpec(memory_space=pltpu.VMEM), out_shape),
        scratch_shapes=list(scratch),
        compiler_params=pltpu.CompilerParams(vmem_limit_bytes=40 * 1024 * 1024),
        cost_estimate=pl.CostEstimate(flops=flops, bytes_accessed=moved, transcendentals=0),
    )(spot, *operands)


def on_device(attn_in, out_grad, o_weight, in_factor, out_factor, store):
    yh, x, z = (lax.axis_index(axis) for axis in DOCS)
    core = lax.axis_index("core")
    tok_rows = out_grad.shape[0]
    rank_size = in_factor.shape[1]
    count = tok_rows // LENGTH
    share = store.shape[1]
    half_width = o_weight.shape[0] // 2
    spot = jnp.stack([yh, x, z]).astype(jnp.int32)

    tie = lax.optimization_barrier

    shard = o_weight.T
    other = fetch(shard, z=HALF_Z)
    right = jnp.dot(out_grad, out_factor, preferred_element_type=jnp.float32)
    right, other = tie((right, other))

    high = z // HALF_Z
    pair = jnp.stack([jnp.where(high == 0, shard, other), jnp.where(high == 0, other, shard)], 0)
    other = fetch(pair, yh=1)
    doc_sq = jnp.sum(store * store, axis=1)
    other, doc_sq = tie((other, doc_sq))
    left = jnp.dot(attn_in, in_factor, preferred_element_type=jnp.float32)
    partial_proj = jnp.einsum(
        "qlr,qls->qrs",
        left.reshape(count, LENGTH, rank_size),
        right.reshape(count, LENGTH, rank_size),
        precision=lax.Precision.HIGHEST,
    ).reshape(count * rank_size * rank_size // LANES, LANES)
    full_proj = partial_proj + fetch(partial_proj, core=1)
    full_proj = full_proj + fetch(full_proj, yl=1)
    full_proj = full_proj.reshape(count, NL * NC, share // LANES, LANES)
    query_sq = jnp.sum(full_proj * full_proj, axis=(1, 2, 3))
    mine = lax.dynamic_index_in_dim(full_proj, lax.axis_index(DIM), 1, keepdims=False)
    unit_rows = mine * lax.rsqrt(query_sq + 1e-06)[:, None, None]
    unit_rows = (unit_rows * float(rank_size)).astype(jnp.float16)
    unit_rows = unit_rows.reshape(1, count * share // LANES, LANES)
    all_rows = lax.all_to_all(
        jnp.broadcast_to(unit_rows, (NY * NX * NZ,) + unit_rows.shape[1:]), DOCS, 0, 0
    )

    both = jnp.stack([jnp.where(yh == 0, pair, other), jnp.where(yh == 0, other, pair)], 0)
    half_line = jax.ShapeDtypeStruct((NX * 2, shard.shape[0], half_width), shard.dtype)
    lines = on_core(
        build_lines,
        (half_line,) * 4,
        spot,
        around(both[..., :half_width], "x") + around(both[..., half_width:], "z"),
        flops=10000000000,
    )
    own_a, own_b = lines[:2], lines[2:]

    first = [
        fetch(own_b[0], x=1), fetch(own_b[1], x=-1), fetch(own_a[0], z=1), fetch(own_a[1], z=-1)
    ]
    second = [
        fetch(own_b[0], x=-1), fetch(own_b[1], x=1), fetch(own_a[0], z=-1), fetch(own_a[1], z=1)
    ]
    all_rows, *first = tie((all_rows, *first))
    all_rows = all_rows.reshape(NY * NX * NZ * count, share).astype(jnp.float32)
    far_b = [fetch(first[0], x=1), fetch(first[1], x=-1)]
    far_a = [fetch(first[2], z=1), fetch(first[3], z=-1)]

    partial_scores = lax.dot_general(
        all_rows,
        store,
        (((1,), (1,)), ((), ())),
        precision=lax.Precision.HIGH,
        preferred_element_type=jnp.float32,
    )
    half = partial_scores.shape[0] // NC
    norm_rows = jnp.broadcast_to(doc_sq[None, :], (8, doc_sq.shape[0]))
    kept = lax.dynamic_slice_in_dim(partial_scores, core * half, half, 0)
    given = lax.dynamic_slice_in_dim(partial_scores, (1 - core) * half, half, 0)
    kept = jnp.concatenate([kept, norm_rows], 0)
    given = jnp.concatenate([given, norm_rows], 0)
    kept = kept + fetch(given, core=1)
    kept, *second = tie((kept, *second))
    up_a, down_a = (first[2], second[3]), (second[2], first[3])
    up_b, down_b = (first[0], second[1]), (second[0], first[1])
    kept = kept + fetch(kept, yl=1)
    kept = kept[:half] * lax.rsqrt(kept[half] + 1e-06)[None, :]
    other = fetch(kept, core=1)
    scores = jnp.concatenate(
        [jnp.where(core == 0, kept, other), jnp.where(core == 0, other, kept)], 0
    )

    def weights(*parts):
        depth = out_grad.shape[1]
        return [pltpu.VMEM((depth * part // 4, half_width), out_grad.dtype) for part in parts]

    sums = jax.ShapeDtypeStruct((tok_rows, half_width), jnp.float32)
    flops = 2 * tok_rows * out_grad.shape[1] * half_width
    sum_a, sum_b = on_core(
        near_part,
        (sums, sums),
        spot,
        [out_grad, *own_a, *up_a, *down_a, *own_b, *up_b, *down_b],
        weights(2, 3),
        flops * 5 // 4,
    )
    in_cotangent = on_core(
        far_part,
        jax.ShapeDtypeStruct((tok_rows, 2 * half_width), out_grad.dtype),
        spot,
        [out_grad, sum_a, sum_b, *up_a, *down_a, *far_a, *far_b],
        weights(2, 1),
        flops * 3 // 4,
    )
    return (in_cotangent, scores)


def solution(mesh):
    mesh = Mesh(mesh.devices.reshape(NY, NX, NZ, NL, NC), NAMES)
    placed = (
        P(DOCS, DIM),
        P(DOCS, None),
        P(DIM, DOCS),
        P(DIM, None),
        P(),
        P(DOCS, DIM),
    )
    return jax.shard_map(
        on_device,
        mesh=mesh,
        in_specs=placed,
        out_specs=(P(DOCS, DIM), P(None, DOCS)),
        check_vma=False,
    )
```

```python
import functools

import jax
import jax.numpy as jnp
from jax import lax
from jax.experimental import pallas as pl
from jax.experimental.pallas import tpu as pltpu
from jax.sharding import Mesh
from jax.sharding import PartitionSpec as P

LENGTH = 256
NY, NX, NZ, NL, NC = 2, 4, 8, 2, 2
NAMES = ("yh", "x", "z", "yl", "core")
SIZES = dict(zip(NAMES, (NY, NX, NZ, NL, NC)))
DOCS = ("yh", "x", "z")
DIM = ("yl", "core")
LANES = 128
HALF_Z = NZ // 2


def fetch(value, **shift):
    ((axis, by),) = shift.items()
    size = SIZES[axis]
    return lax.ppermute(value, axis, [((to + by) % size, to) for to in range(size)])


HOPS = (0, 3, 1, 2)


def around(block, axis):
    if axis == "z":
        pairs = [((to + (-2 if to % 2 else 2)) % NZ, to) for to in range(NZ)]
        far = lax.ppermute(block, axis, pairs)
    else:
        far = fetch(block, **{axis: 2})
    return [block, fetch(block, **{axis: -1}), fetch(block, **{axis: 1}), far]


STEP = 384


def build_lines(spot_ref, *refs):
    x, low = spot_ref[1], spot_ref[2] & (HALF_Z - 1)
    for index, hop in enumerate(HOPS):
        at_x, at_z = (x + hop) & (NX - 1), (low + hop) & (HALF_Z - 1)
        for at_y in range(NY):
            for high in range(2):
                refs[8 + at_y][at_x * 2 + high] = refs[index][at_y, high]
                refs[10 + at_y][high * HALF_Z + at_z] = refs[4 + index][at_y, high]


def place_a(weight, halves, bit):
    depth = halves[0].shape[1]
    for at_y, half in enumerate(halves):
        for block in range(half.shape[0]):
            start = ((at_y * half.shape[0] + block) * 2 + bit) * depth
            weight[pl.ds(pl.multiple_of(start, depth), depth), :] = half[block]


def place_b(weight, halves):
    depth = halves[0].shape[1]
    for index, half in enumerate(halves):
        for block in range(half.shape[0]):
            start = (index * half.shape[0] + block) * depth
            weight[start : start + depth, :] = half[block]


def product_a(grad_ref, rows, weight, tile):
    columns = []
    for part in range(NY * NX * 2):
        start = part * 2 * LANES + tile * LANES
        columns.append(grad_ref[rows, pl.ds(pl.multiple_of(start, LANES), LANES)])
    return jnp.dot(
        jnp.concatenate(columns, 1), weight[...], preferred_element_type=jnp.float32
    )


def product_b(grad_ref, rows, weight, at_xs):
    half = weight.shape[0] // (NY * len(at_xs))
    columns = []
    for at_x in at_xs:
        for at_y in range(NY):
            start = (at_y * NX + at_x) * half
            columns.append(grad_ref[rows, pl.ds(pl.multiple_of(start, half), half)])
    return jnp.dot(
        jnp.concatenate(columns, 1), weight[...], preferred_element_type=jnp.float32
    )


def over_rows(grad_ref, body):
    @pl.loop(0, grad_ref.shape[0] // STEP)
    def _(i):
        body(pl.ds(pl.multiple_of(i * STEP, STEP), STEP))


def near_part(spot_ref, grad_ref, *refs):
    own_a, up_a, down_a, own_b, up_b, down_b = (refs[i : i + 2] for i in range(0, 12, 2))
    sum_a, sum_b, weight_a, weight_b = refs[12:]
    x, z = spot_ref[1], spot_ref[2]
    bit = z & 1
    place_a(weight_a, own_a, bit)

    @pl.when(bit == 0)
    def _():
        place_a(weight_a, up_a, 1)

    @pl.when(bit == 1)
    def _():
        place_a(weight_a, down_a, 0)

    place_b(weight_b, (*own_b, *up_b, *down_b))

    def first(rows):
        sum_a[rows, :] = product_a(grad_ref, rows, weight_a, (z >> 1) & 1)
        at_xs = [(x + hop) & (NX - 1) for hop in (0, 1, 3)]
        sum_b[rows, :] = product_b(grad_ref, rows, weight_b, at_xs)

    over_rows(grad_ref, first)


def far_part(spot_ref, grad_ref, sum_a, sum_b, *refs):
    up_a, down_a, far_a, far_b = (refs[i : i + 2] for i in range(0, 8, 2))
    out_ref, weight_a, weight_b = refs[8:]
    x, z = spot_ref[1], spot_ref[2]
    width = weight_a.shape[1]
    bit = z & 1
    place_a(weight_a, far_a, bit)

    @pl.when(bit == 0)
    def _():
        place_a(weight_a, down_a, 1)

    @pl.when(bit == 1)
    def _():
        place_a(weight_a, up_a, 0)

    place_b(weight_b, far_b)

    def last(rows):
        part = product_a(grad_ref, rows, weight_a, 1 - ((z >> 1) & 1))
        out_ref[rows, :width] = (sum_a[rows, :] + part).astype(out_ref.dtype)
        part = product_b(grad_ref, rows, weight_b, [(x + 2) & (NX - 1)])
        out_ref[rows, width:] = (sum_b[rows, :] + part).astype(out_ref.dtype)

    over_rows(grad_ref, last)


def on_core(kernel, out_shape, spot, operands, scratch=(), flops=0):
    moved = sum(x.size * x.dtype.itemsize for x in operands)
    return pl.pallas_call(
        kernel,
        out_shape=out_shape,
        in_specs=[pl.BlockSpec(memory_space=pltpu.SMEM)]
        + [pl.BlockSpec(memory_space=pltpu.VMEM)] * len(operands),
        out_specs=jax.tree.map(lambda _: pl.BlockSpec(memory_space=pltpu.VMEM), out_shape),
        scratch_shapes=list(scratch),
        compiler_params=pltpu.CompilerParams(vmem_limit_bytes=40 * 1024 * 1024),
        cost_estimate=pl.CostEstimate(flops=flops, bytes_accessed=moved, transcendentals=0),
    )(spot, *operands)


def on_device(attn_in, out_grad, o_weight, in_factor, out_factor, store):
    yh, x, z = (lax.axis_index(axis) for axis in DOCS)
    core = lax.axis_index("core")
    tok_rows = out_grad.shape[0]
    rank_size = in_factor.shape[1]
    count = tok_rows // LENGTH
    share = store.shape[1]
    half_width = o_weight.shape[0] // 2
    spot = jnp.stack([yh, x, z]).astype(jnp.int32)

    tie = lax.optimization_barrier

    shard = o_weight.T
    other = fetch(shard, z=HALF_Z)
    right = jnp.dot(out_grad, out_factor, preferred_element_type=jnp.float32)
    right, other = tie((right, other))

    high = z // HALF_Z
    pair = jnp.stack([jnp.where(high == 0, shard, other), jnp.where(high == 0, other, shard)], 0)
    other = fetch(pair, yh=1)
    doc_sq = jnp.sum(store * store, axis=1)
    other, doc_sq = tie((other, doc_sq))
    left = jnp.dot(attn_in, in_factor, preferred_element_type=jnp.float32)
    partial_proj = jnp.einsum(
        "qlr,qls->qrs",
        left.reshape(count, LENGTH, rank_size),
        right.reshape(count, LENGTH, rank_size),
        precision=lax.Precision.HIGHEST,
    ).reshape(count * rank_size * rank_size // LANES, LANES)
    full_proj = partial_proj + fetch(partial_proj, core=1)
    full_proj = full_proj + fetch(full_proj, yl=1)
    full_proj = full_proj.reshape(count, NL * NC, share // LANES, LANES)
    query_sq = jnp.sum(full_proj * full_proj, axis=(1, 2, 3))
    mine = lax.dynamic_index_in_dim(full_proj, lax.axis_index(DIM), 1, keepdims=False)
    unit_rows = mine * lax.rsqrt(query_sq + 1e-06)[:, None, None]
    unit_rows = (unit_rows * float(rank_size)).astype(jnp.float16)
    unit_rows = unit_rows.reshape(1, count * share // LANES, LANES)
    rows = lax.all_to_all(
        jnp.broadcast_to(unit_rows, (NY * NZ,) + unit_rows.shape[1:]), ("yh", "z"), 0, 0
    )

    both = jnp.stack([jnp.where(yh == 0, pair, other), jnp.where(yh == 0, other, pair)], 0)
    pieces = around(both[..., :half_width], "x") + around(both[..., half_width:], "z")
    rows, pieces = tie((rows, pieces))
    all_rows = lax.all_to_all(jnp.broadcast_to(rows[None], (NX,) + rows.shape), "x", 0, 0)
    half_line = jax.ShapeDtypeStruct((NX * 2, shard.shape[0], half_width), shard.dtype)
    lines = on_core(
        build_lines,
        (half_line,) * 4,
        spot,
        pieces,
        flops=10000000000,
    )
    own_a, own_b = lines[:2], lines[2:]

    first = [
        fetch(own_b[0], x=1), fetch(own_b[1], x=-1), fetch(own_a[0], z=1), fetch(own_a[1], z=-1)
    ]
    second = [
        fetch(own_b[0], x=-1), fetch(own_b[1], x=1), fetch(own_a[0], z=-1), fetch(own_a[1], z=1)
    ]
    all_rows, *first = tie((all_rows, *first))
    all_rows = jnp.swapaxes(all_rows.reshape((NX, NY, -1) + all_rows.shape[2:]), 0, 1)
    all_rows = all_rows.reshape(NY * NX * NZ * count, share).astype(jnp.float32)
    far_b = [fetch(first[0], x=1), fetch(first[1], x=-1)]
    far_a = [fetch(first[2], z=1), fetch(first[3], z=-1)]

    partial_scores = lax.dot_general(
        all_rows,
        store,
        (((1,), (1,)), ((), ())),
        precision=lax.Precision.HIGH,
        preferred_element_type=jnp.float32,
    )
    half = partial_scores.shape[0] // NC
    norm_rows = jnp.broadcast_to(doc_sq[None, :], (8, doc_sq.shape[0]))
    kept = lax.dynamic_slice_in_dim(partial_scores, core * half, half, 0)
    given = lax.dynamic_slice_in_dim(partial_scores, (1 - core) * half, half, 0)
    kept = jnp.concatenate([kept, norm_rows], 0)
    given = jnp.concatenate([given, norm_rows], 0)
    kept = kept + fetch(given, core=1)
    kept, *second = tie((kept, *second))
    up_a, down_a = (first[2], second[3]), (second[2], first[3])
    up_b, down_b = (first[0], second[1]), (second[0], first[1])
    kept = kept + fetch(kept, yl=1)
    kept = kept[:half] * lax.rsqrt(kept[half] + 1e-06)[None, :]
    other = fetch(kept, core=1)
    scores = jnp.concatenate(
        [jnp.where(core == 0, kept, other), jnp.where(core == 0, other, kept)], 0
    )

    def weights(*parts):
        depth = out_grad.shape[1]
        return [pltpu.VMEM((depth * part // 4, half_width), out_grad.dtype) for part in parts]

    sums = jax.ShapeDtypeStruct((tok_rows, half_width), jnp.float32)
    flops = 2 * tok_rows * out_grad.shape[1] * half_width
    sum_a, sum_b = on_core(
        near_part,
        (sums, sums),
        spot,
        [out_grad, *own_a, *up_a, *down_a, *own_b, *up_b, *down_b],
        weights(2, 3),
        flops * 5 // 4,
    )
    in_cotangent = on_core(
        far_part,
        jax.ShapeDtypeStruct((tok_rows, 2 * half_width), out_grad.dtype),
        spot,
        [out_grad, sum_a, sum_b, *up_a, *down_a, *far_a, *far_b],
        weights(2, 1),
        flops * 3 // 4,
    )
    return (in_cotangent, scores)


def solution(mesh):
    mesh = Mesh(mesh.devices.reshape(NY, NX, NZ, NL, NC), NAMES)
    placed = (
        P(DOCS, DIM),
        P(DOCS, None),
        P(DIM, DOCS),
        P(DIM, None),
        P(),
        P(DOCS, DIM),
    )
    return jax.shard_map(
        on_device,
        mesh=mesh,
        in_specs=placed,
        out_specs=(P(DOCS, DIM), P(None, DOCS)),
        check_vma=False,
    )
```

```python
import functools

import jax
import jax.numpy as jnp
from jax import lax
from jax.experimental import pallas as pl
from jax.experimental.pallas import tpu as pltpu
from jax.sharding import Mesh
from jax.sharding import PartitionSpec as P

LENGTH = 256
NY, NX, NZ, NL, NC = 2, 4, 8, 2, 2
NAMES = ("yh", "x", "z", "yl", "core")
SIZES = dict(zip(NAMES, (NY, NX, NZ, NL, NC)))
DOCS = ("yh", "x", "z")
DIM = ("yl", "core")
LANES = 128
HALF_Z = NZ // 2


def fetch(value, **shift):
    ((axis, by),) = shift.items()
    size = SIZES[axis]
    return lax.ppermute(value, axis, [((to + by) % size, to) for to in range(size)])


HOPS = (0, 3, 1, 2)


def around(block, axis):
    if axis == "z":
        pairs = [((to + (-2 if to % 2 else 2)) % NZ, to) for to in range(NZ)]
        far = lax.ppermute(block, axis, pairs)
    else:
        far = fetch(block, **{axis: 2})
    return [block, fetch(block, **{axis: -1}), fetch(block, **{axis: 1}), far]


STEP = 384


def spread(spot_ref, row_ref, out_ref):
    out_ref[...] = jnp.broadcast_to(row_ref[...], out_ref.shape)


def build_lines(spot_ref, *refs):
    x, low = spot_ref[1], spot_ref[2] & (HALF_Z - 1)
    for index, hop in enumerate(HOPS):
        at_x, at_z = (x + hop) & (NX - 1), (low + hop) & (HALF_Z - 1)
        for at_y in range(NY):
            for high in range(2):
                refs[8 + at_y][at_x * 2 + high] = refs[index][at_y, high]
                refs[10 + at_y][high * HALF_Z + at_z] = refs[4 + index][at_y, high]


def place_a(weight, halves, bit):
    depth = halves[0].shape[1]
    for at_y, half in enumerate(halves):
        for block in range(half.shape[0]):
            start = ((at_y * half.shape[0] + block) * 2 + bit) * depth
            weight[pl.ds(pl.multiple_of(start, depth), depth), :] = half[block]


def place_b(weight, halves):
    depth = halves[0].shape[1]
    for index, half in enumerate(halves):
        for block in range(half.shape[0]):
            start = (index * half.shape[0] + block) * depth
            weight[start : start + depth, :] = half[block]


def product_a(grad_ref, rows, weight, tile):
    columns = []
    for part in range(NY * NX * 2):
        start = part * 2 * LANES + tile * LANES
        columns.append(grad_ref[rows, pl.ds(pl.multiple_of(start, LANES), LANES)])
    return jnp.dot(
        jnp.concatenate(columns, 1), weight[...], preferred_element_type=jnp.float32
    )


def product_b(grad_ref, rows, weight, at_xs):
    half = weight.shape[0] // (NY * len(at_xs))
    columns = []
    for at_x in at_xs:
        for at_y in range(NY):
            start = (at_y * NX + at_x) * half
            columns.append(grad_ref[rows, pl.ds(pl.multiple_of(start, half), half)])
    return jnp.dot(
        jnp.concatenate(columns, 1), weight[...], preferred_element_type=jnp.float32
    )


def over_rows(grad_ref, body):
    @pl.loop(0, grad_ref.shape[0] // STEP)
    def _(i):
        body(pl.ds(pl.multiple_of(i * STEP, STEP), STEP))


def near_part(spot_ref, grad_ref, *refs):
    own_a, up_a, down_a, own_b, up_b, down_b = (refs[i : i + 2] for i in range(0, 12, 2))
    sum_a, sum_b, weight_a, weight_b = refs[12:]
    x, z = spot_ref[1], spot_ref[2]
    bit = z & 1
    place_a(weight_a, own_a, bit)

    @pl.when(bit == 0)
    def _():
        place_a(weight_a, up_a, 1)

    @pl.when(bit == 1)
    def _():
        place_a(weight_a, down_a, 0)

    place_b(weight_b, (*own_b, *up_b, *down_b))

    def first(rows):
        sum_a[rows, :] = product_a(grad_ref, rows, weight_a, (z >> 1) & 1)
        at_xs = [(x + hop) & (NX - 1) for hop in (0, 1, 3)]
        sum_b[rows, :] = product_b(grad_ref, rows, weight_b, at_xs)

    over_rows(grad_ref, first)


def far_part(spot_ref, grad_ref, sum_a, sum_b, *refs):
    up_a, down_a, far_a, far_b = (refs[i : i + 2] for i in range(0, 8, 2))
    out_ref, weight_a, weight_b = refs[8:]
    x, z = spot_ref[1], spot_ref[2]
    width = weight_a.shape[1]
    bit = z & 1
    place_a(weight_a, far_a, bit)

    @pl.when(bit == 0)
    def _():
        place_a(weight_a, down_a, 1)

    @pl.when(bit == 1)
    def _():
        place_a(weight_a, up_a, 0)

    place_b(weight_b, far_b)

    def last(rows):
        part = product_a(grad_ref, rows, weight_a, 1 - ((z >> 1) & 1))
        out_ref[rows, :width] = (sum_a[rows, :] + part).astype(out_ref.dtype)
        part = product_b(grad_ref, rows, weight_b, [(x + 2) & (NX - 1)])
        out_ref[rows, width:] = (sum_b[rows, :] + part).astype(out_ref.dtype)

    over_rows(grad_ref, last)


def on_core(kernel, out_shape, spot, operands, scratch=(), flops=0):
    moved = sum(x.size * x.dtype.itemsize for x in operands)
    return pl.pallas_call(
        kernel,
        out_shape=out_shape,
        in_specs=[pl.BlockSpec(memory_space=pltpu.SMEM)]
        + [pl.BlockSpec(memory_space=pltpu.VMEM)] * len(operands),
        out_specs=jax.tree.map(lambda _: pl.BlockSpec(memory_space=pltpu.VMEM), out_shape),
        scratch_shapes=list(scratch),
        compiler_params=pltpu.CompilerParams(vmem_limit_bytes=40 * 1024 * 1024),
        cost_estimate=pl.CostEstimate(flops=flops, bytes_accessed=moved, transcendentals=0),
    )(spot, *operands)


def on_device(attn_in, out_grad, o_weight, in_factor, out_factor, store):
    yh, x, z = (lax.axis_index(axis) for axis in DOCS)
    core = lax.axis_index("core")
    tok_rows = out_grad.shape[0]
    rank_size = in_factor.shape[1]
    count = tok_rows // LENGTH
    share = store.shape[1]
    half_width = o_weight.shape[0] // 2
    spot = jnp.stack([yh, x, z]).astype(jnp.int32)

    tie = lax.optimization_barrier

    shard = o_weight.T
    other = fetch(shard, z=HALF_Z)
    right = jnp.dot(out_grad, out_factor, preferred_element_type=jnp.float32)
    right, other = tie((right, other))

    high = z // HALF_Z
    pair = jnp.stack([jnp.where(high == 0, shard, other), jnp.where(high == 0, other, shard)], 0)
    other = fetch(pair, yh=1)
    doc_sq = jnp.sum(store * store, axis=1)
    other, doc_sq = tie((other, doc_sq))
    left = jnp.dot(attn_in, in_factor, preferred_element_type=jnp.float32)
    partial_proj = jnp.einsum(
        "qlr,qls->qrs",
        left.reshape(count, LENGTH, rank_size),
        right.reshape(count, LENGTH, rank_size),
        precision=lax.Precision.HIGHEST,
    ).reshape(count * rank_size * rank_size // LANES, LANES)
    full_proj = partial_proj + fetch(partial_proj, core=1)
    full_proj = full_proj + fetch(full_proj, yl=1)
    full_proj = full_proj.reshape(count, NL * NC, share // LANES, LANES)
    query_sq = jnp.sum(full_proj * full_proj, axis=(1, 2, 3))
    mine = lax.dynamic_index_in_dim(full_proj, lax.axis_index(DIM), 1, keepdims=False)
    unit_rows = mine * lax.rsqrt(query_sq + 1e-06)[:, None, None]
    unit_rows = (unit_rows * float(rank_size)).astype(jnp.float16)
    unit_rows = unit_rows.reshape(1, count * share // LANES, LANES)
    all_rows = lax.all_to_all(
        jnp.broadcast_to(unit_rows, (NY * NX * NZ,) + unit_rows.shape[1:]), DOCS, 0, 0
    )

    both = jnp.stack([jnp.where(yh == 0, pair, other), jnp.where(yh == 0, other, pair)], 0)
    half_line = jax.ShapeDtypeStruct((NX * 2, shard.shape[0], half_width), shard.dtype)
    lines = on_core(
        build_lines,
        (half_line,) * 4,
        spot,
        around(both[..., :half_width], "x") + around(both[..., half_width:], "z"),
        flops=10000000000,
    )
    own_a, own_b = lines[:2], lines[2:]

    first = [
        fetch(own_b[0], x=1), fetch(own_b[1], x=-1), fetch(own_a[0], z=1), fetch(own_a[1], z=-1)
    ]
    second = [
        fetch(own_b[0], x=-1), fetch(own_b[1], x=1), fetch(own_a[0], z=-1), fetch(own_a[1], z=1)
    ]
    doc_sq, *first = tie((doc_sq, *first))
    norm_rows = jax.ShapeDtypeStruct((8, doc_sq.shape[0]), jnp.float32)
    norm_rows = on_core(spread, norm_rows, spot, [doc_sq[None, :]], flops=8000000000)
    all_rows, norm_rows = tie((all_rows, norm_rows))
    all_rows = all_rows.reshape(NY * NX * NZ * count, share).astype(jnp.float32)
    far_b = [fetch(first[0], x=1), fetch(first[1], x=-1)]
    far_a = [fetch(first[2], z=1), fetch(first[3], z=-1)]

    partial_scores = lax.dot_general(
        all_rows,
        store,
        (((1,), (1,)), ((), ())),
        precision=lax.Precision.HIGH,
        preferred_element_type=jnp.float32,
    )
    half = partial_scores.shape[0] // NC
    kept = lax.dynamic_slice_in_dim(partial_scores, core * half, half, 0)
    given = lax.dynamic_slice_in_dim(partial_scores, (1 - core) * half, half, 0)
    kept = jnp.concatenate([kept, norm_rows], 0)
    given = jnp.concatenate([given, norm_rows], 0)
    kept = kept + fetch(given, core=1)
    kept, *second = tie((kept, *second))
    up_a, down_a = (first[2], second[3]), (second[2], first[3])
    up_b, down_b = (first[0], second[1]), (second[0], first[1])
    kept = kept + fetch(kept, yl=1)
    kept = kept[:half] * lax.rsqrt(kept[half] + 1e-06)[None, :]
    other = fetch(kept, core=1)
    scores = jnp.concatenate(
        [jnp.where(core == 0, kept, other), jnp.where(core == 0, other, kept)], 0
    )

    def weights(*parts):
        depth = out_grad.shape[1]
        return [pltpu.VMEM((depth * part // 4, half_width), out_grad.dtype) for part in parts]

    sums = jax.ShapeDtypeStruct((tok_rows, half_width), jnp.float32)
    flops = 2 * tok_rows * out_grad.shape[1] * half_width
    sum_a, sum_b = on_core(
        near_part,
        (sums, sums),
        spot,
        [out_grad, *own_a, *up_a, *down_a, *own_b, *up_b, *down_b],
        weights(2, 3),
        flops * 5 // 4,
    )
    in_cotangent = on_core(
        far_part,
        jax.ShapeDtypeStruct((tok_rows, 2 * half_width), out_grad.dtype),
        spot,
        [out_grad, sum_a, sum_b, *up_a, *down_a, *far_a, *far_b],
        weights(2, 1),
        flops * 3 // 4,
    )
    return (in_cotangent, scores)


def solution(mesh):
    mesh = Mesh(mesh.devices.reshape(NY, NX, NZ, NL, NC), NAMES)
    placed = (
        P(DOCS, DIM),
        P(DOCS, None),
        P(DIM, DOCS),
        P(DIM, None),
        P(),
        P(DOCS, DIM),
    )
    return jax.shard_map(
        on_device,
        mesh=mesh,
        in_specs=placed,
        out_specs=(P(DOCS, DIM), P(None, DOCS)),
        check_vma=False,
    )
```

```python
import functools

import jax
import jax.numpy as jnp
from jax import lax
from jax.experimental import pallas as pl
from jax.experimental.pallas import tpu as pltpu
from jax.sharding import Mesh
from jax.sharding import PartitionSpec as P

LENGTH = 256
NY, NX, NZ, NL, NC = 2, 4, 8, 2, 2
NAMES = ("yh", "x", "z", "yl", "core")
SIZES = dict(zip(NAMES, (NY, NX, NZ, NL, NC)))
DOCS = ("yh", "x", "z")
DIM = ("yl", "core")
LANES = 128
HALF_Z = NZ // 2


def fetch(value, **shift):
    ((axis, by),) = shift.items()
    size = SIZES[axis]
    return lax.ppermute(value, axis, [((to + by) % size, to) for to in range(size)])


HOPS = (0, 3, 1, 2)


def around(block, axis):
    if axis == "z":
        pairs = [((to + (-2 if to % 2 else 2)) % NZ, to) for to in range(NZ)]
        far = lax.ppermute(block, axis, pairs)
    else:
        far = fetch(block, **{axis: 2})
    return [block, fetch(block, **{axis: -1}), fetch(block, **{axis: 1}), far]


STEP = 384


def build_lines(spot_ref, *refs):
    x, low = spot_ref[1], spot_ref[2] & (HALF_Z - 1)
    for index, hop in enumerate(HOPS):
        at_x, at_z = (x + hop) & (NX - 1), (low + hop) & (HALF_Z - 1)
        for at_y in range(NY):
            for high in range(2):
                refs[8 + at_y][at_x * 2 + high] = refs[2 * index][at_y, high]
                refs[10 + at_y][high * HALF_Z + at_z] = refs[2 * index + 1][at_y, high]


def place_a(weight, halves, bit):
    depth = halves[0].shape[1]
    for at_y, half in enumerate(halves):
        for block in range(half.shape[0]):
            start = ((at_y * half.shape[0] + block) * 2 + bit) * depth
            weight[pl.ds(pl.multiple_of(start, depth), depth), :] = half[block]


def place_b(weight, halves):
    depth = halves[0].shape[1]
    for index, half in enumerate(halves):
        for block in range(half.shape[0]):
            start = (index * half.shape[0] + block) * depth
            weight[start : start + depth, :] = half[block]


def product_a(grad_ref, rows, weight, tile):
    columns = []
    for part in range(NY * NX * 2):
        start = part * 2 * LANES + tile * LANES
        columns.append(grad_ref[rows, pl.ds(pl.multiple_of(start, LANES), LANES)])
    return jnp.dot(
        jnp.concatenate(columns, 1), weight[...], preferred_element_type=jnp.float32
    )


def product_b(grad_ref, rows, weight, at_xs):
    half = weight.shape[0] // (NY * len(at_xs))
    columns = []
    for at_x in at_xs:
        for at_y in range(NY):
            start = (at_y * NX + at_x) * half
            columns.append(grad_ref[rows, pl.ds(pl.multiple_of(start, half), half)])
    return jnp.dot(
        jnp.concatenate(columns, 1), weight[...], preferred_element_type=jnp.float32
    )


def over_rows(grad_ref, body):
    @pl.loop(0, grad_ref.shape[0] // STEP)
    def _(i):
        body(pl.ds(pl.multiple_of(i * STEP, STEP), STEP))


def near_part(spot_ref, grad_ref, *refs):
    own_a, up_a, down_a, own_b, up_b, down_b = (refs[i : i + 2] for i in range(0, 12, 2))
    sum_a, sum_b, weight_a, weight_b = refs[12:]
    x, z = spot_ref[1], spot_ref[2]
    bit = z & 1
    place_a(weight_a, own_a, bit)

    @pl.when(bit == 0)
    def _():
        place_a(weight_a, up_a, 1)

    @pl.when(bit == 1)
    def _():
        place_a(weight_a, down_a, 0)

    place_b(weight_b, (*own_b, *up_b, *down_b))

    def first(rows):
        sum_a[rows, :] = product_a(grad_ref, rows, weight_a, (z >> 1) & 1)
        at_xs = [(x + hop) & (NX - 1) for hop in (0, 1, 3)]
        sum_b[rows, :] = product_b(grad_ref, rows, weight_b, at_xs)

    over_rows(grad_ref, first)


def far_part(spot_ref, grad_ref, sum_a, sum_b, *refs):
    up_a, down_a, far_a, far_b = (refs[i : i + 2] for i in range(0, 8, 2))
    out_ref, weight_a, weight_b = refs[8:]
    x, z = spot_ref[1], spot_ref[2]
    width = weight_a.shape[1]
    bit = z & 1
    place_a(weight_a, far_a, bit)

    @pl.when(bit == 0)
    def _():
        place_a(weight_a, down_a, 1)

    @pl.when(bit == 1)
    def _():
        place_a(weight_a, up_a, 0)

    place_b(weight_b, far_b)

    def last(rows):
        part = product_a(grad_ref, rows, weight_a, 1 - ((z >> 1) & 1))
        out_ref[rows, :width] = (sum_a[rows, :] + part).astype(out_ref.dtype)
        part = product_b(grad_ref, rows, weight_b, [(x + 2) & (NX - 1)])
        out_ref[rows, width:] = (sum_b[rows, :] + part).astype(out_ref.dtype)

    over_rows(grad_ref, last)


def on_core(kernel, out_shape, spot, operands, scratch=(), flops=0):
    moved = sum(x.size * x.dtype.itemsize for x in operands)
    return pl.pallas_call(
        kernel,
        out_shape=out_shape,
        in_specs=[pl.BlockSpec(memory_space=pltpu.SMEM)]
        + [pl.BlockSpec(memory_space=pltpu.VMEM)] * len(operands),
        out_specs=jax.tree.map(lambda _: pl.BlockSpec(memory_space=pltpu.VMEM), out_shape),
        scratch_shapes=list(scratch),
        compiler_params=pltpu.CompilerParams(vmem_limit_bytes=40 * 1024 * 1024),
        cost_estimate=pl.CostEstimate(flops=flops, bytes_accessed=moved, transcendentals=0),
    )(spot, *operands)


def on_device(attn_in, out_grad, o_weight, in_factor, out_factor, store):
    yh, x, z = (lax.axis_index(axis) for axis in DOCS)
    core = lax.axis_index("core")
    tok_rows = out_grad.shape[0]
    rank_size = in_factor.shape[1]
    count = tok_rows // LENGTH
    share = store.shape[1]
    half_width = o_weight.shape[0] // 2
    spot = jnp.stack([yh, x, z]).astype(jnp.int32)

    tie = lax.optimization_barrier

    shard = o_weight.T
    other = fetch(shard, z=HALF_Z)
    right = jnp.dot(out_grad, out_factor, preferred_element_type=jnp.float32)
    right, other = tie((right, other))

    high = z // HALF_Z
    pair = jnp.stack([jnp.where(high == 0, shard, other), jnp.where(high == 0, other, shard)], 0)
    other = fetch(pair, yh=1)
    doc_sq = jnp.sum(store * store, axis=1)
    other, doc_sq = tie((other, doc_sq))
    left = jnp.dot(attn_in, in_factor, preferred_element_type=jnp.float32)
    partial_proj = jnp.einsum(
        "qlr,qls->qrs",
        left.reshape(count, LENGTH, rank_size),
        right.reshape(count, LENGTH, rank_size),
        precision=lax.Precision.HIGHEST,
    ).reshape(count * rank_size * rank_size // LANES, LANES)
    full_proj = partial_proj + fetch(partial_proj, core=1)
    full_proj = full_proj + fetch(full_proj, yl=1)
    full_proj = full_proj.reshape(count, NL * NC, share // LANES, LANES)
    query_sq = jnp.sum(full_proj * full_proj, axis=(1, 2, 3))
    mine = lax.dynamic_index_in_dim(full_proj, lax.axis_index(DIM), 1, keepdims=False)
    unit_rows = mine * lax.rsqrt(query_sq + 1e-06)[:, None, None]
    unit_rows = (unit_rows * float(rank_size)).astype(jnp.float16)
    unit_rows = unit_rows.reshape(1, count * share // LANES, LANES)
    all_rows = lax.all_to_all(
        jnp.broadcast_to(unit_rows, (NY * NX * NZ,) + unit_rows.shape[1:]), DOCS, 0, 0
    )

    both = jnp.stack([jnp.where(yh == 0, pair, other), jnp.where(yh == 0, other, pair)], 0)
    from_x, from_z = around(both[..., :half_width], "x"), around(both[..., half_width:], "z")
    half_line = jax.ShapeDtypeStruct((NX * 2, shard.shape[0], half_width), shard.dtype)
    lines = on_core(
        build_lines,
        (half_line,) * 4,
        spot,
        [block for both_ways in zip(from_x, from_z) for block in both_ways],
        flops=10000000000,
    )
    own_a, own_b = lines[:2], lines[2:]

    first = [
        fetch(own_b[0], x=1), fetch(own_b[1], x=-1), fetch(own_a[0], z=1), fetch(own_a[1], z=-1)
    ]
    second = [
        fetch(own_b[0], x=-1), fetch(own_b[1], x=1), fetch(own_a[0], z=-1), fetch(own_a[1], z=1)
    ]
    all_rows, *first = tie((all_rows, *first))
    all_rows = all_rows.reshape(NY * NX * NZ * count, share).astype(jnp.float32)
    far_b = [fetch(first[0], x=1), fetch(first[1], x=-1)]
    far_a = [fetch(first[2], z=1), fetch(first[3], z=-1)]

    partial_scores = lax.dot_general(
        all_rows,
        store,
        (((1,), (1,)), ((), ())),
        precision=lax.Precision.HIGH,
        preferred_element_type=jnp.float32,
    )
    half = partial_scores.shape[0] // NC
    norm_rows = jnp.broadcast_to(doc_sq[None, :], (8, doc_sq.shape[0]))
    kept = lax.dynamic_slice_in_dim(partial_scores, core * half, half, 0)
    given = lax.dynamic_slice_in_dim(partial_scores, (1 - core) * half, half, 0)
    kept = jnp.concatenate([kept, norm_rows], 0)
    given = jnp.concatenate([given, norm_rows], 0)
    kept = kept + fetch(given, core=1)
    kept, *second = tie((kept, *second))
    up_a, down_a = (first[2], second[3]), (second[2], first[3])
    up_b, down_b = (first[0], second[1]), (second[0], first[1])
    kept = kept + fetch(kept, yl=1)
    kept = kept[:half] * lax.rsqrt(kept[half] + 1e-06)[None, :]
    other = fetch(kept, core=1)
    mine_first = lax.broadcasted_iota(jnp.int32, (NC,) + kept.shape, 0) == core
    scores = jnp.where(mine_first, kept[None], other[None]).reshape(NC * half, -1)

    def weights(*parts):
        depth = out_grad.shape[1]
        return [pltpu.VMEM((depth * part // 4, half_width), out_grad.dtype) for part in parts]

    sums = jax.ShapeDtypeStruct((tok_rows, half_width), jnp.float32)
    flops = 2 * tok_rows * out_grad.shape[1] * half_width
    sum_a, sum_b = on_core(
        near_part,
        (sums, sums),
        spot,
        [out_grad, *own_a, *up_a, *down_a, *own_b, *up_b, *down_b],
        weights(2, 3),
        flops * 5 // 4,
    )
    in_cotangent = on_core(
        far_part,
        jax.ShapeDtypeStruct((tok_rows, 2 * half_width), out_grad.dtype),
        spot,
        [out_grad, sum_a, sum_b, *up_a, *down_a, *far_a, *far_b],
        weights(2, 1),
        flops * 3 // 4,
    )
    return (in_cotangent, scores)


def solution(mesh):
    mesh = Mesh(mesh.devices.reshape(NY, NX, NZ, NL, NC), NAMES)
    placed = (
        P(DOCS, DIM),
        P(DOCS, None),
        P(DIM, DOCS),
        P(DIM, None),
        P(),
        P(DOCS, DIM),
    )
    return jax.shard_map(
        on_device,
        mesh=mesh,
        in_specs=placed,
        out_specs=(P(DOCS, DIM), P(None, DOCS)),
        check_vma=False,
    )
```
